32 devices in a mesh: grp: 2 (over y), lon: 8 (over z, x), lat: 2 (over core).
Axes of the slice: x: 2, y: 2, z: 4, core: 2. Of those that a mesh axis runs over, the one named last changes fastest.
Arguments:
- state: float32 [5, 192, 64], P(None, ('grp', 'lon'), 'lat'), parts along dimension 1, may hold values from -4 to 4
- target: float32 [5, 192, 64], P(None, ('grp', 'lon'), 'lat'), parts along dimension 1, may hold values from -4 to 4
- depth: float32 [192, 64], P(('grp', 'lon'), 'lat'), parts along dimension 0, may hold values from 0.5 to 1.5
- land_mask: int32 [192, 64], P(('grp', 'lon'), 'lat'), parts along dimension 0, may hold values from 0 to 1, as said below
- w_one: float32 [45, 256], replicated, may hold values from -0.875 to 0.875
- b_one: float32 [256], replicated, may hold values from -3 to 3
- w_two: float32 [256, 256], replicated, may hold values from -0.375 to 0.375
- b_two: float32 [256], replicated, may hold values from -3 to 3
- w_three: float32 [256, 5], replicated, may hold values from -0.375 to 0.375
- b_three: float32 [5], replicated, may hold values from -3 to 3
Outputs:
- loss_value: float32 [2], P('grp'), parts along dimension 0
- state_adjoint: float32 [5, 192, 64], P(None, ('grp', 'lon'), 'lat'), parts along dimension 1
- direction_w_one: float32 [90, 256], P('grp'), parts along dimension 0
- direction_b_one: float32 [512], P('grp'), parts along dimension 0
- direction_w_two: float32 [512, 256], P('grp'), parts along dimension 0
- direction_b_two: float32 [512], P('grp'), parts along dimension 0
- direction_w_three: float32 [512, 5], P('grp'), parts along dimension 0
- direction_b_three: float32 [10], P('grp'), parts along dimension 0
The draws below stay inside these ranges and needn't reach their ends.
There are 2 independent parts, one for each index of `grp`. The reference program is written for one: setup_inputs(seed, part) draws one part's arguments, and reference() takes and returns one part's arrays. A program takes and returns all parts, laid end to end along the dimension named above; an argument that names none is the same for every part. Nothing has to cross between parts.
Inputs may be any that keep to these rules, and one draw needn't show every extreme that they name: `land_mask`: land is drawn cell by cell; in alternate eighths of the longitudes about 70 and about 15 percent of the cells are land.
All inputs are finite; a program needn't handle non-finite values.
Results may differ from the reference program's by a relative error of at most 0.0001.
Values sent between devices are 32-bit elements; how exact they have to be, the bound alone decides.
A program may use at most 64 MiB of HBM per device.

```python
import jax
import jax.numpy as jnp
from jax import lax

FIELDS = 5
FEATS = 45
HIDDEN_SIZE = 256
STEPS = 2
NLON = 96
NLAT = 64


def draw_land_mask(key, part):
    noise = jax.random.randint(key, (NLON, NLAT), 0, 100)
    bands = jnp.arange(NLON, dtype=jnp.int32) * 8 // NLON % 2
    limits = 15 + 55 * bands
    return (noise < limits[:, None]).astype(jnp.int32)


def steps_of(own_key, shape, cuts, smallest, top_value):
    level, own = 1.0, jax.random.fold_in(own_key, 6)
    for dim, parts in cuts:
        draws = jnp.exp(jax.random.uniform(jax.random.fold_in(own, dim), (parts,), jnp.float32, smallest / len(cuts), top_value / len(cuts)))
        level = level * jnp.repeat(draws, shape[dim] // parts).reshape([-1 if axis == dim else 1 for axis in range(len(shape))])
    return level


def gaussian(own_key, dims, width, most, pieces=(), held_as=jnp.bfloat16):
    drawn = width * jax.random.normal(own_key, dims, jnp.float32)
    if pieces:
        drawn = drawn * steps_of(own_key, dims, pieces, -0.22, 0.18)
    return jnp.clip(drawn, -most, most).astype(held_as)


def setup_inputs(seed: int = 0, part: int = 0) -> dict:
    keys = jax.random.split(jax.random.key(seed), 11)
    part_splits = jax.random.split(jax.random.fold_in(keys[10], part), 11)
    return {
        "state": gaussian(part_splits[0], (FIELDS, NLON, NLAT), 1.0, 4.0, ((1, 8), (2, 2)), jnp.float32),
        "target": gaussian(part_splits[1], (FIELDS, NLON, NLAT), 1.0, 4.0, ((1, 8), (2, 2)), jnp.float32),
        "depth": jnp.clip(0.5 + 1.0 * jax.random.uniform(part_splits[2], (NLON, NLAT), jnp.float32) ** steps_of(part_splits[2], (NLON, NLAT), ((0, 8), (1, 2)), -0.2, 0.2), 0.5, 1.5),
        "land_mask": draw_land_mask(jax.random.fold_in(jax.random.fold_in(keys[10], part), 71), part),
        "w_one": gaussian(keys[4], (FEATS, HIDDEN_SIZE), FEATS ** -0.5, 0.875, (), jnp.float32),
        "b_one": gaussian(keys[5], (HIDDEN_SIZE,), 0.5, 3.0, (), jnp.float32),
        "w_two": gaussian(keys[6], (HIDDEN_SIZE, HIDDEN_SIZE), HIDDEN_SIZE ** -0.5, 0.375, (), jnp.float32),
        "b_two": gaussian(keys[7], (HIDDEN_SIZE,), 0.5, 3.0, (), jnp.float32),
        "w_three": gaussian(keys[8], (HIDDEN_SIZE, FIELDS), HIDDEN_SIZE ** -0.5, 0.375, (), jnp.float32),
        "b_three": gaussian(keys[9], (FIELDS,), 0.5, 3.0, (), jnp.float32),
    }


time_step = 0.4
gravity = 1.0
drag_rate = 0.05
viscosity = 0.05
diffusion = 0.05
eps_norm = 1e-06

def closure(padded, weights):
    w_one, b_one, w_two, b_two, w_three, b_three = weights
    channels, width_lon, width_lat = padded.shape
    inner_lon = width_lon - 2
    inner_lat = width_lat - 2
    shifted = [padded[:, offset_lon:offset_lon + inner_lon, offset_lat:offset_lat + inner_lat] for offset_lon in range(3) for offset_lat in range(3)]
    features = jnp.concatenate(shifted, axis=0).reshape(9 * channels, inner_lon * inner_lat)
    hidden_one = jnp.tanh(jnp.dot(w_one.T, features, precision=lax.Precision.HIGHEST, preferred_element_type=jnp.float32) + b_one[:, None])
    hidden_two = jnp.tanh(jnp.dot(w_two.T, hidden_one, precision=lax.Precision.HIGHEST, preferred_element_type=jnp.float32) + b_two[:, None])
    output = jnp.dot(w_three.T, hidden_two, precision=lax.Precision.HIGHEST, preferred_element_type=jnp.float32) + b_three[:, None]
    return output.reshape(channels, inner_lon, inner_lat)

def tendency(padded, fixed, coriolis, weights):
    centre_cells = padded[:, 1:-1, 1:-1]
    eastward = padded[:, 2:, 1:-1]
    westward = padded[:, :-2, 1:-1]
    northward = padded[:, 1:-1, 2:]
    southward = padded[:, 1:-1, :-2]
    laplace = eastward + westward + northward + southward - 4.0 * centre_cells
    column_depth = fixed[1]
    flux_lon = column_depth * padded[1]
    flux_lat = column_depth * padded[2]
    divergence = 0.5 * (flux_lon[2:, 1:-1] - flux_lon[:-2, 1:-1] + flux_lat[1:-1, 2:] - flux_lat[1:-1, :-2])
    speed_u = centre_cells[1]
    speed_v = centre_cells[2]
    rate_height = -divergence
    rate_u = coriolis * speed_v - gravity * 0.5 * (eastward[0] - westward[0]) - drag_rate * speed_u + viscosity * laplace[1]
    rate_v = -coriolis * speed_u - gravity * 0.5 * (northward[0] - southward[0]) - drag_rate * speed_v + viscosity * laplace[2]
    rate_tracer = -0.5 * (speed_u * (eastward[3:] - westward[3:]) + speed_v * (northward[3:] - southward[3:])) + diffusion * laplace[3:]
    rates = jnp.concatenate([rate_height[None], rate_u[None], rate_v[None], rate_tracer], axis=0)
    return (rates + closure(padded, weights)) * fixed[0, 1:-1, 1:-1]

def advance(section_level, inner, start, rates):
    if section_level == 0:
        return inner + time_step * rates
    if section_level == 1:
        return 0.75 * start + 0.25 * (inner + time_step * rates)
    return 1.0 / 3.0 * start + 2.0 / 3.0 * (inner + time_step * rates)

def wrap_pad(field):
    wrapped = jnp.concatenate([field[:, -1:], field, field[:, :1]], axis=1)
    return jnp.pad(wrapped, ((0, 0), (0, 0), (1, 1)))

def reference(state, target, depth, land_mask, w_one, b_one, w_two, b_two, w_three, b_three):
    ocean = (1 - land_mask).astype(jnp.float32)
    fixed = wrap_pad(jnp.stack([ocean, depth]))
    latitudes = jnp.arange(NLAT, dtype=jnp.int32).astype(jnp.float32)
    coriolis = 0.2 + 0.6 * (latitudes + 0.5) / NLAT

    def misfit_of(initial, weights):
        current = initial * ocean
        for step_index in range(STEPS):
            start = current
            for section_level in range(3):
                rates = tendency(wrap_pad(current), fixed, coriolis, weights)
                current = advance(section_level, current, start, rates)
        error = current - target
        return 0.5 * jnp.sum(ocean * error * error)
    misfit, pullback = jax.vjp(misfit_of, state, (w_one, b_one, w_two, b_two, w_three, b_three))
    state_adjoint, grads = pullback(jnp.ones_like(misfit))
    total = sum((jnp.sum(grad * grad) for grad in grads))
    number = sum((grad.size for grad in grads))
    scale = 1.0 / jnp.sqrt(total / number + eps_norm)
    loss_value = (misfit / (NLON * NLAT)).reshape(1)
    return (loss_value, state_adjoint, grads[0] * scale, grads[1] * scale, grads[2] * scale, grads[3] * scale, grads[4] * scale, grads[5] * scale)
```

```python
import functools

import jax
import jax.numpy as jnp
from jax import lax
from jax.experimental import pallas as pl
from jax.experimental.pallas import tpu as pltpu
from jax.sharding import PartitionSpec as P

STEPS = 2
LEVELS = 3 * STEPS
HID = 256
FROWS = 80
time_step = 0.4
eps_norm = 1e-06
f32 = jnp.float32
bf16 = jnp.bfloat16
MESH = pl.DeviceIdType.MESH


def split(value):
    high = value.astype(bf16)
    low = (value - high.astype(f32)).astype(bf16)
    return high, low


def matmul(left, right):
    return jnp.dot(left, right, preferred_element_type=f32)


def matmul_t(left, right):
    return lax.dot_general(left, right, (((1,), (1,)), ((), ())), preferred_element_type=f32)


def stacked(value):
    high, low = split(value)
    return jnp.concatenate([high, low, high], axis=0)


def kernel(
    peers, chunk, row, number, cells_total,
    field_ref, w1_ref, w2_ref, w3t_ref, b2_ref, b3_ref,
    loss_out, adj_out, w1_out, b1_out, w2_out, b2_out, w3_out, b3_out,
    part_buf, edge_send, edge_recv, tape_f, tape_h1, tape_h2,
    w1_fwd, w1_bwd, w2_fwd, w2_bwd, w3_fwd, w3_bwd,
    acc_w1, acc_w2, acc_w3, acc_b2, acc_b3,
    grad_buf, reduce_buf, gather_buf,
    part_sem, edge_ssem, edge_rsem, back_sem, rs_ssem, rs_rsem, ag_ssem, ag_rsem,
):
    grp = lax.axis_index("grp")
    lon = lax.axis_index("lon")
    half = lax.axis_index("lat")
    me = lon * 2 + half

    def place(position):
        return (grp, position // 2, position % 2)

    east = place((me + 1) % peers)
    west = place((me + peers - 1) % peers)
    partner = (grp, lon, 1 - half)

    barrier = pltpu.get_barrier_semaphore()

    def greet(step, carry):
        pl.semaphore_signal(barrier, inc=1, device_id=place((me + step) % peers), device_id_type=MESH)
        return carry

    lax.fori_loop(1, peers, greet, 0, unroll=peers <= 16)
    pl.semaphore_wait(barrier, peers - 1)

    first = pltpu.make_async_remote_copy(
        src_ref=field_ref.at[1 - half], dst_ref=part_buf,
        send_sem=part_sem.at[0], recv_sem=part_sem.at[1],
        device_id=partner, device_id_type=MESH,
    )
    first.start()

    lanes = field_ref.shape[2]
    lane = lax.broadcasted_iota(jnp.int32, (8, lanes), 1)
    sub = lax.broadcasted_iota(jnp.int32, (8, lanes), 0)
    latitude = lane % row
    low_edge = latitude == 0
    high_edge = latitude == row - 1
    lane_tile = lax.broadcasted_iota(jnp.int32, (8, 128), 1)
    lower_half = lane_tile < row
    coriolis = (0.2 + 0.6 * (latitude.astype(f32) + 0.5) / row)[0:1]

    w1 = w1_ref[...]
    high, low = split(w1)
    w1_bwd[...] = jnp.concatenate([high, high, low], axis=1)
    high, low = high.astype(f32), low.astype(f32)
    w1_fwd[...] = jnp.concatenate([high, high, low], axis=0).T.astype(bf16)
    w2 = w2_ref[...]
    high, low = split(w2)
    w2_bwd[...] = jnp.concatenate([high, high, low], axis=1)
    high, low = split(w2.T)
    w2_fwd[...] = jnp.concatenate([high, high, low], axis=1)
    w3t = w3t_ref[...]
    high, low = split(w3t)
    w3_fwd[...] = jnp.concatenate([high, high, low], axis=1)
    high, low = high.astype(f32)[:8], low.astype(f32)[:8]
    w3_bwd[...] = jnp.concatenate([high, high, low, jnp.zeros_like(low)], axis=0).T.astype(bf16)
    acc_w1[...] = jnp.zeros_like(acc_w1)
    acc_w2[...] = jnp.zeros_like(acc_w2)
    acc_w3[...] = jnp.zeros_like(acc_w3)
    acc_b2[...] = jnp.zeros_like(acc_b2)
    acc_b3[...] = jnp.zeros_like(acc_b3)

    first.wait()
    merged = field_ref[half] + part_buf[...]
    fields = merged[:8]
    target = merged[8:]
    ocean = fields[6:7]
    state0 = jnp.where(sub < 5, fields * ocean, fields)

    def exchange(stage, to_east, to_west):
        edge_send[stage, 0] = to_east
        edge_send[stage, 1] = to_west
        copies = []
        for side, device in ((0, east), (1, west)):
            copy = pltpu.make_async_remote_copy(
                src_ref=edge_send.at[stage, side], dst_ref=edge_recv.at[stage, side],
                send_sem=edge_ssem.at[stage, side], recv_sem=edge_rsem.at[stage, side],
                device_id=device, device_id_type=MESH,
            )
            copy.start()
            copies.append(copy)
        return copies

    def lat_down(value):
        return jnp.where(low_edge, 0.0, pltpu.roll(value, 1, 1))

    def lat_up(value):
        return jnp.where(high_edge, 0.0, pltpu.roll(value, lanes - 1, 1))

    def factors(level):
        keep = jnp.where(level == 0, 0.0, jnp.where(level == 1, 0.75, 1.0 / 3.0)).astype(f32)
        move = jnp.where(level == 0, 1.0, jnp.where(level == 1, 0.25, 2.0 / 3.0)).astype(f32)
        return keep, move

    ones_group = jnp.where(sub == 0, 1.0, 0.0).astype(f32)

    def forward(stage, carry):
        current, start = carry
        level = stage % 3
        start = jnp.where(level == 0, current, start)
        from_west = pltpu.roll(current, row, 1)
        from_east = pltpu.roll(current, lanes - row, 1)
        copies = exchange(stage, from_west[:, :128], from_east[:, lanes - 128 :])
        centre = [lat_down(current), current, lat_up(current)]
        for copy in copies:
            copy.wait()
        west_side = jnp.concatenate(
            [jnp.where(lower_half, edge_recv[stage, 0], from_west[:, :128]), from_west[:, 128:]], axis=1
        )
        east_side = jnp.concatenate(
            [
                from_east[:, : lanes - 128],
                jnp.where(lower_half, from_east[:, lanes - 128 :], edge_recv[stage, 1]),
            ],
            axis=1,
        )
        groups = (
            [lat_down(west_side), west_side, lat_up(west_side)]
            + centre
            + [lat_down(east_side), east_side, lat_up(east_side)]
        )
        feats = jnp.concatenate(groups + [ones_group], axis=0)
        tape_f[stage] = feats
        hidden_one = jnp.tanh(matmul(w1_fwd[...], stacked(feats)))
        tape_h1[stage] = hidden_one
        hidden_two = jnp.tanh(matmul(w2_fwd[...], stacked(hidden_one)) + b2_ref[...])
        tape_h2[stage] = hidden_two
        closure = matmul(w3_fwd[...], stacked(hidden_two))[:8] + b3_ref[...]
        we, ea, so, no = groups[1], groups[7], groups[3], groups[5]
        laplace = ea + we + no + so - 4.0 * current
        dx, dy = ea - we, no - so
        u, v = current[1:2], current[2:3]
        rate_h = -0.5 * (ea[5:6] * ea[1:2] - we[5:6] * we[1:2] + no[5:6] * no[2:3] - so[5:6] * so[2:3])
        rate_u = coriolis * v - 0.5 * dx[0:1] - 0.05 * u + 0.05 * laplace[1:2]
        rate_v = -coriolis * u - 0.5 * dy[0:1] - 0.05 * v + 0.05 * laplace[2:3]
        rate_t = 0.05 * laplace - 0.5 * (u * dx + v * dy)
        rates = jnp.where(sub == 0, rate_h, jnp.where(sub == 1, rate_u, jnp.where(sub == 2, rate_v, rate_t)))
        rates = (rates + closure) * ocean
        keep, move = factors(level)
        moved = keep * start + move * (current + time_step * rates)
        return jnp.where(sub < 5, moved, current), start

    final, _ = lax.fori_loop(0, LEVELS, forward, (state0, state0))
    error = jnp.where(sub < 5, final - target, 0.0)
    adjoint = ocean * error
    misfit = 0.5 * jnp.sum(jnp.sum(adjoint * error, axis=1, keepdims=True), axis=0, keepdims=True)

    def backward(index, carry):
        adjoint, start_total = carry
        stage = LEVELS - 1 - index
        slot = LEVELS + index
        level = stage % 3
        keep, move = factors(level)
        start_total = jnp.where(level == 2, 0.0, start_total) + keep * adjoint
        grad = (move * time_step) * adjoint * ocean
        feats = tape_f[stage]
        hidden_one = tape_h1[stage]
        hidden_two = tape_h2[stage]
        high, low = split(grad)
        high, low = high.astype(f32), low.astype(f32)
        grad_stack = jnp.concatenate([high, low, high, jnp.zeros_like(high)], axis=0).astype(bf16)
        dz2 = matmul(w3_bwd[...], grad_stack) * (1.0 - hidden_two * hidden_two)
        dz2_high, dz2_low = split(dz2)
        dz1 = matmul(w2_bwd[...], jnp.concatenate([dz2_high, dz2_low, dz2_high], axis=0)) * (
            1.0 - hidden_one * hidden_one
        )
        dz1_high, dz1_low = split(dz1)
        dfeats = matmul(w1_bwd[...], jnp.concatenate([dz1_high, dz1_low, dz1_high], axis=0))
        we, ea, so, no, ce = feats[8:16], feats[56:64], feats[24:32], feats[40:48], feats[32:40]
        dx, dy = ea - we, no - so
        u, v = ce[1:2], ce[2:3]
        gh, gu, gv = grad[0:1], grad[1:2], grad[2:3]
        gt = jnp.where(sub >= 3, grad, 0.0)
        lap = jnp.where(sub >= 1, 0.05 * grad, 0.0)
        ugt, vgt = u * gt, v * gt
        d_ea = lap - 0.5 * jnp.where(sub == 0, gu, jnp.where(sub == 1, gh * ea[5:6], ugt))
        d_we = lap + 0.5 * jnp.where(sub == 0, gu, jnp.where(sub == 1, gh * we[5:6], ugt))
        d_no = lap - 0.5 * jnp.where(sub == 0, gv, jnp.where(sub == 2, gh * no[5:6], vgt))
        d_so = lap + 0.5 * jnp.where(sub == 0, gv, jnp.where(sub == 2, gh * so[5:6], vgt))
        du = -coriolis * gv - 0.05 * gu - 0.5 * jnp.sum(gt * dx, axis=0, keepdims=True)
        dv = coriolis * gu - 0.05 * gv - 0.5 * jnp.sum(gt * dy, axis=0, keepdims=True)
        d_ce = jnp.where(sub == 1, du, jnp.where(sub == 2, dv, 0.0)) - 4.0 * lap
        part = [dfeats[8 * i : 8 * i + 8] for i in range(9)]
        to_west = lat_up(part[0]) + (part[1] + d_we) + lat_down(part[2])
        to_east = lat_up(part[6]) + (part[7] + d_ea) + lat_down(part[8])
        stay = lat_up(part[3] + d_so) + (part[4] + d_ce) + lat_down(part[5] + d_no)
        to_west = pltpu.roll(to_west, lanes - row, 1)
        to_east = pltpu.roll(to_east, row, 1)
        copies = exchange(
            slot,
            jnp.where(lower_half, to_east[:, :128], 0.0),
            jnp.where(lower_half, 0.0, to_west[:, lanes - 128 :]),
        )
        result = (
            move * adjoint
            + stay
            + jnp.where(lane < row, 0.0, to_east)
            + jnp.where(lane >= lanes - row, 0.0, to_west)
        )
        h1_high, h1_low = split(hidden_one)
        acc_w2[...] += matmul_t(
            jnp.concatenate([h1_high, h1_high, h1_low], axis=1),
            jnp.concatenate([dz2_high, dz2_low, dz2_high], axis=1),
        )
        f_high, f_low = split(feats)
        acc_w1[...] += matmul_t(
            jnp.concatenate([f_high, f_high, f_low], axis=1),
            jnp.concatenate([dz1_high, dz1_low, dz1_high], axis=1),
        )
        h2_high, h2_low = split(hidden_two)
        g16 = jnp.concatenate([grad, jnp.zeros_like(grad)], axis=0)
        g_high, g_low = split(g16)
        acc_w3[...] += matmul_t(
            jnp.concatenate([g_high, g_high, g_low], axis=1),
            jnp.concatenate([h2_high, h2_low, h2_high], axis=1),
        )[:8]
        acc_b2[...] += sum(dz2[:, i : i + 128] for i in range(0, lanes, 128))
        acc_b3[...] += sum(grad[:, i : i + 128] for i in range(0, lanes, 128))
        for copy in copies:
            copy.wait()
        result = jnp.concatenate(
            [result[:, :128] + edge_recv[slot, 0]]
            + [result[:, i : i + 128] for i in range(128, lanes - 128, 128)]
            + [result[:, lanes - 128 :] + edge_recv[slot, 1]],
            axis=1,
        )
        result = jnp.where(level == 0, result + start_total, result)
        return result, start_total

    adjoint, _ = lax.fori_loop(0, LEVELS, backward, (adjoint, jnp.zeros_like(adjoint)))
    adj_out[half] = adjoint * ocean

    f_row = lax.broadcasted_iota(jnp.int32, (FROWS, HID), 0)
    real = ((f_row < 72) & (f_row % 8 < 5)) | (f_row == 72)
    sub_w = lax.broadcasted_iota(jnp.int32, (8, HID), 0)
    lane_w = lax.broadcasted_iota(jnp.int32, (8, HID), 1)
    b2_row = jnp.sum(acc_b2[...].T, axis=0, keepdims=True)
    b3_col = jnp.sum(acc_b3[...], axis=1, keepdims=True)
    tile_b2 = jnp.where(sub_w == 0, b2_row, 0.0)
    tile_b3 = jnp.where(lane_w == 0, jnp.where(sub_w == 5, misfit, jnp.where(sub_w < 5, b3_col, 0.0)), 0.0)
    extra = peers * chunk - (HID + FROWS + 24)
    pieces = [acc_w2[...], jnp.where(real, acc_w1[...], 0.0), acc_w3[...], tile_b2, tile_b3]
    if extra:
        pieces.append(jnp.zeros((extra, HID), f32))
    grad_buf[...] = jnp.concatenate(pieces, axis=0).reshape(peers, chunk, HID)

    back = pltpu.make_async_remote_copy(
        src_ref=adj_out.at[half], dst_ref=adj_out.at[half],
        send_sem=back_sem.at[0], recv_sem=back_sem.at[1],
        device_id=partner, device_id_type=MESH,
    )

    def scatter(step):
        to = (me + step) % peers
        return pltpu.make_async_remote_copy(
            src_ref=grad_buf.at[to], dst_ref=reduce_buf.at[step],
            send_sem=rs_ssem.at[step], recv_sem=rs_rsem.at[step],
            device_id=place(to), device_id_type=MESH,
        )

    def gather(step):
        to = (me + step) % peers
        return pltpu.make_async_remote_copy(
            src_ref=gather_buf.at[me], dst_ref=gather_buf.at[me],
            send_sem=ag_ssem.at[step], recv_sem=ag_rsem.at[step],
            device_id=place(to), device_id_type=MESH,
        )

    def loop(body, init):
        return lax.fori_loop(1, peers, body, init, unroll=peers <= 16)

    def start_of(make):
        def body(step, carry):
            make(step).start()
            return carry

        return body

    loop(start_of(scatter), 0)
    back.start()

    def take(step, total):
        scatter(step).wait_recv()
        return total + reduce_buf[step]

    gather_buf[me] = loop(take, grad_buf[me])
    loop(start_of(gather), 0)

    def arrive(step, carry):
        source = (me + peers - step) % peers
        pltpu.make_async_remote_copy(
            src_ref=gather_buf.at[source], dst_ref=gather_buf.at[source],
            send_sem=ag_ssem.at[step], recv_sem=ag_rsem.at[step],
            device_id=place((me + step) % peers), device_id_type=MESH,
        ).wait_recv()
        return carry

    loop(arrive, 0)
    summed = gather_buf[...].reshape(peers * chunk, HID)
    base = HID + FROWS + 16
    is_loss = (sub_w == 5) & (lane_w == 0)
    last = summed[base : base + 8]
    square = summed[:base] * summed[:base]
    total = jnp.sum(jnp.sum(square, axis=0, keepdims=True), axis=1, keepdims=True)
    rest = jnp.where(is_loss, 0.0, last * last)
    total = total + jnp.sum(jnp.sum(rest, axis=0, keepdims=True), axis=1, keepdims=True)
    scale = 1.0 / jnp.sqrt(total / number + eps_norm)
    w2_out[...] = summed[:HID] * scale
    for i in range(9):
        w1_out[5 * i : 5 * i + 5] = summed[HID + 8 * i : HID + 8 * i + 5] * scale
    b1_out[...] = summed[HID + 72 : HID + 73] * scale
    w3_out[...] = (summed[HID + FROWS : HID + FROWS + 8] * scale).T[:, :5]
    b2_out[...] = summed[HID + FROWS + 8 : HID + FROWS + 9] * scale
    b3_out[...] = (last * scale)[:, :1]
    loss_out[...] = last[5:6, :1] / cells_total

    back.wait()

    def drain(step, carry):
        scatter(step).wait_send()
        gather(step).wait_send()
        return carry

    loop(drain, 0)


def on_device(state, target, depth, land_mask, w_one, b_one, w_two, b_two, w_three, b_three):
    half = lax.axis_index("lat")
    halves = lax.axis_size("lat")
    peers = lax.axis_size("lon") * halves
    cells_lon, cells_lat = depth.shape
    row = cells_lat * halves
    lines = cells_lon // halves
    lanes = lines * row
    ocean = (1 - land_mask).astype(f32)
    zero = jnp.zeros((1, cells_lon, cells_lat), f32)
    block = jnp.concatenate(
        [state, depth[None], ocean[None], zero, target, jnp.zeros((3, cells_lon, cells_lat), f32)], axis=0
    )
    block = jnp.concatenate(
        [jnp.where(half == 0, block, 0.0), jnp.where(half == 1, block, 0.0)], axis=2
    )
    fields = block.reshape(16, halves, lanes).transpose(1, 0, 2)
    w1 = jnp.pad(w_one.reshape(9, 5, HID), ((0, 0), (0, 3), (0, 0))).reshape(72, HID)
    w1 = jnp.concatenate([w1, b_one[None], jnp.zeros((FROWS - 73, HID), f32)], axis=0)
    w3t = jnp.pad(w_three.T, ((0, 11), (0, 0)))
    b2 = b_two[:, None]
    b3 = jnp.pad(b_three, (0, 3))[:, None]
    number = w_one.size + b_one.size + w_two.size + b_two.size + w_three.size + b_three.size
    used = HID + FROWS + 24
    chunk = -(-used // peers)
    chunk = -(-chunk // 8) * 8
    shape = jax.ShapeDtypeStruct
    vmem = pl.BlockSpec(memory_space=pltpu.VMEM)
    dma = pltpu.SemaphoreType.DMA
    cells_total = peers // halves * cells_lon * row
    outs = pl.pallas_call(
        functools.partial(kernel, peers, chunk, row, float(number), float(cells_total)),
        out_shape=(
            shape((1, 1), f32), shape((2, 8, lanes), f32), shape((45, HID), f32), shape((1, HID), f32),
            shape((HID, HID), f32), shape((1, HID), f32), shape((HID, 5), f32), shape((8, 1), f32),
        ),
        in_specs=[vmem] * 6,
        out_specs=(vmem,) * 8,
        scratch_shapes=[
            pltpu.VMEM((16, lanes), f32),
            pltpu.VMEM((2 * LEVELS, 2, 8, 128), f32),
            pltpu.VMEM((2 * LEVELS, 2, 8, 128), f32),
            pltpu.VMEM((LEVELS, FROWS, lanes), f32),
            pltpu.VMEM((LEVELS, HID, lanes), f32),
            pltpu.VMEM((LEVELS, HID, lanes), f32),
            pltpu.VMEM((HID, 3 * FROWS), bf16),
            pltpu.VMEM((FROWS, 3 * HID), bf16),
            pltpu.VMEM((HID, 3 * HID), bf16),
            pltpu.VMEM((HID, 3 * HID), bf16),
            pltpu.VMEM((16, 3 * HID), bf16),
            pltpu.VMEM((HID, 32), bf16),
            pltpu.VMEM((FROWS, HID), f32),
            pltpu.VMEM((HID, HID), f32),
            pltpu.VMEM((8, HID), f32),
            pltpu.VMEM((HID, 128), f32),
            pltpu.VMEM((8, 128), f32),
            pltpu.VMEM((peers, chunk, HID), f32),
            pltpu.VMEM((peers, chunk, HID), f32),
            pltpu.VMEM((peers, chunk, HID), f32),
            dma((2,)),
            dma((2 * LEVELS, 2)),
            dma((2 * LEVELS, 2)),
            dma((2,)),
            dma((peers,)),
            dma((peers,)),
            dma((peers,)),
            dma((peers,)),
        ],
        compiler_params=pltpu.CompilerParams(
            collective_id=0, has_side_effects=True, vmem_limit_bytes=40 * 1024 * 1024
        ),
    )(fields, w1, w_two, w3t, b2, b3)
    loss, adjoint, d1, e1, d2, e2, d3, e3 = outs
    adjoint = adjoint[:, :5].reshape(2, 5, lines, row).transpose(1, 0, 2, 3).reshape(5, cells_lon, row)
    adjoint = jnp.where(half == 0, adjoint[:, :, :cells_lat], adjoint[:, :, cells_lat:])
    return (
        loss.reshape(1), adjoint, d1, e1.reshape(HID), d2, e2.reshape(HID), d3, e3[:5, 0],
    )


def solution(mesh):
    in_specs = (
        P(None, ("grp", "lon"), "lat"),
        P(None, ("grp", "lon"), "lat"),
        P(("grp", "lon"), "lat"),
        P(("grp", "lon"), "lat"),
    ) + (P(),) * 6
    out_specs = (
        P("grp"),
        P(None, ("grp", "lon"), "lat"),
        P("grp", None),
        P("grp"),
        P("grp", None),
        P("grp"),
        P("grp", None),
        P("grp"),
    )
    return jax.shard_map(
        on_device, mesh=mesh, in_specs=in_specs, out_specs=out_specs, check_vma=False
    )
```

```python
import functools

import jax
import jax.numpy as jnp
from jax import lax
from jax.experimental import pallas as pl
from jax.experimental.pallas import tpu as pltpu
from jax.sharding import PartitionSpec as P

STEPS = 2
LEVELS = 3 * STEPS
HID = 256
FROWS = 80
time_step = 0.4
eps_norm = 1e-06
f32 = jnp.float32
bf16 = jnp.bfloat16
MESH = pl.DeviceIdType.MESH


def split(value):
    high = value.astype(bf16)
    low = (value - high.astype(f32)).astype(bf16)
    return high, low


def matmul(left, right):
    return jnp.dot(left, right, preferred_element_type=f32)


def matmul_t(left, right):
    return lax.dot_general(left, right, (((1,), (1,)), ((), ())), preferred_element_type=f32)


def stacked(value):
    high, low = split(value)
    return jnp.concatenate([high, low, high], axis=0)


def kernel(
    peers, chunk, row, number, cells_total,
    field_ref, w1_ref, b1_ref, w2_ref, b2_ref, w3_ref, b3_ref,
    loss_out, adj_out, w1_out, b1_out, w2_out, b2_out, w3_out, b3_out,
    w1_pad, w3_pad, b2_col, adj_src, part_buf, edge_send, edge_recv, tape_f, tape_h1, tape_h2,
    w1_fwd, w1_bwd, w2_fwd, w2_bwd, w3_fwd, w3_bwd,
    acc_w1, acc_w2, acc_w3, acc_b2, acc_b3,
    grad_buf, reduce_buf, gather_buf,
    part_ssem, part_rsem, edge_ssem, edge_rsem, back_ssem, back_rsem, rs_ssem, rs_rsem, ag_ssem, ag_rsem,
):
    grp = lax.axis_index("grp")
    lon = lax.axis_index("lon")
    half = lax.axis_index("lat")
    snake = peers == 16

    def chip_at(spot):
        return jnp.where(spot < 4, 2 * spot, 15 - 2 * spot) if snake else spot

    spot = jnp.where(lon % 2 == 0, lon // 2, 7 - lon // 2) if snake else lon
    me = spot * 2 + half

    def place(position):
        return (grp, chip_at(position // 2), position % 2)

    east = place((me + 1) % peers)
    west = place((me + peers - 1) % peers)

    barrier = pltpu.get_barrier_semaphore()

    def greet(step, carry):
        pl.semaphore_signal(barrier, inc=1, device_id=place((me + step) % peers), device_id_type=MESH)
        return carry

    lax.fori_loop(1, peers, greet, 0, unroll=peers <= 16)
    pl.semaphore_wait(barrier, peers - 1)

    def spread(side):
        return pltpu.make_async_remote_copy(
            src_ref=field_ref.at[side], dst_ref=part_buf.at[half],
            send_sem=part_ssem.at[side], recv_sem=part_rsem.at[half],
            device_id=(grp, chip_at(lon), side), device_id_type=MESH,
        )

    def arrival(side):
        return pltpu.make_async_remote_copy(
            src_ref=field_ref.at[side], dst_ref=part_buf.at[side],
            send_sem=part_ssem.at[side], recv_sem=part_rsem.at[side],
            device_id=(grp, chip_at(lon), side), device_id_type=MESH,
        )

    at_home = spot == lon

    def remote(side):
        return jnp.logical_not(at_home & (half == side))

    def own(side):
        return at_home & (half == side)

    for side in range(2):
        @pl.when(remote(side))
        def _(side=side):
            spread(side).start()

        @pl.when(own(side))
        def _(side=side):
            part_buf[side] = field_ref[side]

    lanes = field_ref.shape[2]
    lane = lax.broadcasted_iota(jnp.int32, (8, lanes), 1)
    sub = lax.broadcasted_iota(jnp.int32, (8, lanes), 0)
    latitude = lane % row
    low_edge = latitude == 0
    high_edge = latitude == row - 1
    lane_tile = lax.broadcasted_iota(jnp.int32, (8, 128), 1)
    lower_half = lane_tile < row
    coriolis = (0.2 + 0.6 * (latitude.astype(f32) + 0.5) / row)[0:1]

    w1_pad[...] = jnp.zeros_like(w1_pad)
    for i in range(9):
        w1_pad[8 * i : 8 * i + 5] = w1_ref[5 * i : 5 * i + 5]
    w1_pad[72:73] = b1_ref[...]
    w3_pad[...] = jnp.zeros_like(w3_pad)
    w3_pad[:, :5] = w3_ref[...]
    b2_col[...] = jnp.broadcast_to(b2_ref[...], (128, HID)).T
    corner = lax.broadcasted_iota(jnp.int32, (8, 5), 0) == lax.broadcasted_iota(jnp.int32, (8, 5), 1)
    bias_three = jnp.sum(jnp.where(corner, b3_ref[...], 0.0), axis=1, keepdims=True)
    w1 = w1_pad[...]
    high, low = split(w1)
    w1_bwd[...] = jnp.concatenate([high, high, low], axis=1)
    high, low = high.astype(f32), low.astype(f32)
    w1_fwd[...] = jnp.concatenate([high, high, low], axis=0).T.astype(bf16)
    w2 = w2_ref[...]
    high, low = split(w2)
    w2_bwd[...] = jnp.concatenate([high, high, low], axis=1)
    high, low = split(w2.T)
    w2_fwd[...] = jnp.concatenate([high, high, low], axis=1)
    w3t = w3_pad[...].T[:16]
    high, low = split(w3t)
    w3_fwd[...] = jnp.concatenate([high, high, low], axis=1)
    high, low = high.astype(f32)[:8], low.astype(f32)[:8]
    w3_bwd[...] = jnp.concatenate([high, high, low, jnp.zeros_like(low)], axis=0).T.astype(bf16)
    acc_w1[...] = jnp.zeros_like(acc_w1)
    acc_w2[...] = jnp.zeros_like(acc_w2)
    acc_w3[...] = jnp.zeros_like(acc_w3)
    acc_b2[...] = jnp.zeros_like(acc_b2)
    acc_b3[...] = jnp.zeros_like(acc_b3)

    for side in range(2):
        @pl.when(remote(side))
        def _(side=side):
            arrival(side).wait()

    merged = part_buf[0] + part_buf[1]
    fields = merged[:8]
    target = merged[8:]
    ocean = fields[6:7]
    state0 = jnp.where(sub < 5, fields * ocean, fields)

    def exchange(stage, to_east, to_west):
        edge_send[stage, 0] = to_east
        edge_send[stage, 1] = to_west
        copies = []
        for side, device in ((0, east), (1, west)):
            copy = pltpu.make_async_remote_copy(
                src_ref=edge_send.at[stage, side], dst_ref=edge_recv.at[stage, side],
                send_sem=edge_ssem.at[stage, side], recv_sem=edge_rsem.at[stage, side],
                device_id=device, device_id_type=MESH,
            )
            copy.start()
            copies.append(copy)
        return copies

    def lat_down(value):
        return jnp.where(low_edge, 0.0, pltpu.roll(value, 1, 1))

    def lat_up(value):
        return jnp.where(high_edge, 0.0, pltpu.roll(value, lanes - 1, 1))

    def factors(level):
        keep = jnp.where(level == 0, 0.0, jnp.where(level == 1, 0.75, 1.0 / 3.0)).astype(f32)
        move = jnp.where(level == 0, 1.0, jnp.where(level == 1, 0.25, 2.0 / 3.0)).astype(f32)
        return keep, move

    ones_group = jnp.where(sub == 0, 1.0, 0.0).astype(f32)

    def forward(stage, carry):
        current, start = carry
        level = stage % 3
        start = jnp.where(level == 0, current, start)
        from_west = pltpu.roll(current, row, 1)
        from_east = pltpu.roll(current, lanes - row, 1)
        copies = exchange(stage, from_west[:, :128], from_east[:, lanes - 128 :])
        centre = [lat_down(current), current, lat_up(current)]
        for copy in copies:
            copy.wait()
        west_side = jnp.concatenate(
            [jnp.where(lower_half, edge_recv[stage, 0], from_west[:, :128]), from_west[:, 128:]], axis=1
        )
        east_side = jnp.concatenate(
            [
                from_east[:, : lanes - 128],
                jnp.where(lower_half, from_east[:, lanes - 128 :], edge_recv[stage, 1]),
            ],
            axis=1,
        )
        groups = (
            [lat_down(west_side), west_side, lat_up(west_side)]
            + centre
            + [lat_down(east_side), east_side, lat_up(east_side)]
        )
        feats = jnp.concatenate(groups + [ones_group], axis=0)
        tape_f[stage] = feats
        hidden_one = jnp.tanh(matmul(w1_fwd[...], stacked(feats)))
        tape_h1[stage] = hidden_one
        hidden_two = jnp.tanh(matmul(w2_fwd[...], stacked(hidden_one)) + b2_col[:, :1])
        tape_h2[stage] = hidden_two
        closure = matmul(w3_fwd[...], stacked(hidden_two))[:8] + bias_three
        we, ea, so, no = groups[1], groups[7], groups[3], groups[5]
        laplace = ea + we + no + so - 4.0 * current
        dx, dy = ea - we, no - so
        u, v = current[1:2], current[2:3]
        rate_h = -0.5 * (ea[5:6] * ea[1:2] - we[5:6] * we[1:2] + no[5:6] * no[2:3] - so[5:6] * so[2:3])
        rate_u = coriolis * v - 0.5 * dx[0:1] - 0.05 * u + 0.05 * laplace[1:2]
        rate_v = -coriolis * u - 0.5 * dy[0:1] - 0.05 * v + 0.05 * laplace[2:3]
        rate_t = 0.05 * laplace - 0.5 * (u * dx + v * dy)
        rates = jnp.where(sub == 0, rate_h, jnp.where(sub == 1, rate_u, jnp.where(sub == 2, rate_v, rate_t)))
        rates = (rates + closure) * ocean
        keep, move = factors(level)
        moved = keep * start + move * (current + time_step * rates)
        return jnp.where(sub < 5, moved, current), start

    final, _ = lax.fori_loop(0, LEVELS, forward, (state0, state0))
    error = jnp.where(sub < 5, final - target, 0.0)
    adjoint = ocean * error
    misfit = 0.5 * jnp.sum(jnp.sum(adjoint * error, axis=1, keepdims=True), axis=0, keepdims=True)

    def backward(index, carry):
        adjoint, start_total = carry
        stage = LEVELS - 1 - index
        slot = LEVELS + index
        level = stage % 3
        keep, move = factors(level)
        start_total = jnp.where(level == 2, 0.0, start_total) + keep * adjoint
        grad = (move * time_step) * adjoint * ocean
        feats = tape_f[stage]
        hidden_one = tape_h1[stage]
        hidden_two = tape_h2[stage]
        high, low = split(grad)
        high, low = high.astype(f32), low.astype(f32)
        grad_stack = jnp.concatenate([high, low, high, jnp.zeros_like(high)], axis=0).astype(bf16)
        dz2 = matmul(w3_bwd[...], grad_stack) * (1.0 - hidden_two * hidden_two)
        dz2_high, dz2_low = split(dz2)
        dz1 = matmul(w2_bwd[...], jnp.concatenate([dz2_high, dz2_low, dz2_high], axis=0)) * (
            1.0 - hidden_one * hidden_one
        )
        dz1_high, dz1_low = split(dz1)
        dfeats = matmul(w1_bwd[...], jnp.concatenate([dz1_high, dz1_low, dz1_high], axis=0))
        we, ea, so, no, ce = feats[8:16], feats[56:64], feats[24:32], feats[40:48], feats[32:40]
        dx, dy = ea - we, no - so
        u, v = ce[1:2], ce[2:3]
        gh, gu, gv = grad[0:1], grad[1:2], grad[2:3]
        gt = jnp.where(sub >= 3, grad, 0.0)
        lap = jnp.where(sub >= 1, 0.05 * grad, 0.0)
        ugt, vgt = u * gt, v * gt
        d_ea = lap - 0.5 * jnp.where(sub == 0, gu, jnp.where(sub == 1, gh * ea[5:6], ugt))
        d_we = lap + 0.5 * jnp.where(sub == 0, gu, jnp.where(sub == 1, gh * we[5:6], ugt))
        d_no = lap - 0.5 * jnp.where(sub == 0, gv, jnp.where(sub == 2, gh * no[5:6], vgt))
        d_so = lap + 0.5 * jnp.where(sub == 0, gv, jnp.where(sub == 2, gh * so[5:6], vgt))
        du = -coriolis * gv - 0.05 * gu - 0.5 * jnp.sum(gt * dx, axis=0, keepdims=True)
        dv = coriolis * gu - 0.05 * gv - 0.5 * jnp.sum(gt * dy, axis=0, keepdims=True)
        d_ce = jnp.where(sub == 1, du, jnp.where(sub == 2, dv, 0.0)) - 4.0 * lap
        part = [dfeats[8 * i : 8 * i + 8] for i in range(9)]
        to_west = lat_up(part[0]) + (part[1] + d_we) + lat_down(part[2])
        to_east = lat_up(part[6]) + (part[7] + d_ea) + lat_down(part[8])
        stay = lat_up(part[3] + d_so) + (part[4] + d_ce) + lat_down(part[5] + d_no)
        to_west = pltpu.roll(to_west, lanes - row, 1)
        to_east = pltpu.roll(to_east, row, 1)
        copies = exchange(
            slot,
            jnp.where(lower_half, to_east[:, :128], 0.0),
            jnp.where(lower_half, 0.0, to_west[:, lanes - 128 :]),
        )
        result = (
            move * adjoint
            + stay
            + jnp.where(lane < row, 0.0, to_east)
            + jnp.where(lane >= lanes - row, 0.0, to_west)
        )
        h1_high, h1_low = split(hidden_one)
        acc_w2[...] += matmul_t(
            jnp.concatenate([h1_high, h1_high, h1_low], axis=1),
            jnp.concatenate([dz2_high, dz2_low, dz2_high], axis=1),
        )
        f_high, f_low = split(feats)
        acc_w1[...] += matmul_t(
            jnp.concatenate([f_high, f_high, f_low], axis=1),
            jnp.concatenate([dz1_high, dz1_low, dz1_high], axis=1),
        )
        h2_high, h2_low = split(hidden_two)
        g16 = jnp.concatenate([grad, jnp.zeros_like(grad)], axis=0)
        g_high, g_low = split(g16)
        acc_w3[...] += matmul_t(
            jnp.concatenate([g_high, g_high, g_low], axis=1),
            jnp.concatenate([h2_high, h2_low, h2_high], axis=1),
        )[:8]
        acc_b2[...] += sum(dz2[:, i : i + 128] for i in range(0, lanes, 128))
        acc_b3[...] += sum(grad[:, i : i + 128] for i in range(0, lanes, 128))
        for copy in copies:
            copy.wait()
        result = jnp.concatenate(
            [result[:, :128] + edge_recv[slot, 0]]
            + [result[:, i : i + 128] for i in range(128, lanes - 128, 128)]
            + [result[:, lanes - 128 :] + edge_recv[slot, 1]],
            axis=1,
        )
        result = jnp.where(level == 0, result + start_total, result)
        return result, start_total

    adjoint, _ = lax.fori_loop(0, LEVELS, backward, (adjoint, jnp.zeros_like(adjoint)))
    adj_src[...] = adjoint * ocean

    f_row = lax.broadcasted_iota(jnp.int32, (FROWS, HID), 0)
    real = ((f_row < 72) & (f_row % 8 < 5)) | (f_row == 72)
    sub_w = lax.broadcasted_iota(jnp.int32, (8, HID), 0)
    lane_w = lax.broadcasted_iota(jnp.int32, (8, HID), 1)
    b2_row = jnp.sum(acc_b2[...].T, axis=0, keepdims=True)
    b3_col = jnp.sum(acc_b3[...], axis=1, keepdims=True)
    tile_b2 = jnp.where(sub_w == 0, b2_row, 0.0)
    tile_b3 = jnp.where(lane_w == 0, jnp.where(sub_w == 5, misfit, jnp.where(sub_w < 5, b3_col, 0.0)), 0.0)
    extra = peers * chunk - (HID + FROWS + 24)
    pieces = [acc_w2[...], jnp.where(real, acc_w1[...], 0.0), acc_w3[...], tile_b2, tile_b3]
    if extra:
        pieces.append(jnp.zeros((extra, HID), f32))
    grad_buf[...] = jnp.concatenate(pieces, axis=0).reshape(peers, chunk, HID)

    def back(side, slot):
        return pltpu.make_async_remote_copy(
            src_ref=adj_src, dst_ref=adj_out.at[slot],
            send_sem=back_ssem.at[side], recv_sem=back_rsem.at[slot],
            device_id=(grp, spot, side), device_id_type=MESH,
        )

    def scatter(step):
        to = (me + step) % peers
        return pltpu.make_async_remote_copy(
            src_ref=grad_buf.at[to], dst_ref=reduce_buf.at[step],
            send_sem=rs_ssem.at[step], recv_sem=rs_rsem.at[step],
            device_id=place(to), device_id_type=MESH,
        )

    def gather(step):
        to = (me + step) % peers
        return pltpu.make_async_remote_copy(
            src_ref=gather_buf.at[me], dst_ref=gather_buf.at[me],
            send_sem=ag_ssem.at[step], recv_sem=ag_rsem.at[step],
            device_id=place(to), device_id_type=MESH,
        )

    def loop(body, init):
        return lax.fori_loop(1, peers, body, init, unroll=peers <= 16)

    def start_of(make):
        def body(step, carry):
            make(step).start()
            return carry

        return body

    loop(start_of(scatter), 0)
    for side in range(2):
        @pl.when(remote(side))
        def _(side=side):
            back(side, half).start()

        @pl.when(own(side))
        def _(side=side):
            adj_out[side] = adj_src[...]

    def take(step, total):
        scatter(step).wait_recv()
        return total + reduce_buf[step]

    gather_buf[me] = loop(take, grad_buf[me])
    loop(start_of(gather), 0)

    def arrive(step, carry):
        source = (me + peers - step) % peers
        pltpu.make_async_remote_copy(
            src_ref=gather_buf.at[source], dst_ref=gather_buf.at[source],
            send_sem=ag_ssem.at[step], recv_sem=ag_rsem.at[step],
            device_id=place((me + step) % peers), device_id_type=MESH,
        ).wait_recv()
        return carry

    loop(arrive, 0)
    summed = gather_buf[...].reshape(peers * chunk, HID)
    base = HID + FROWS + 16
    is_loss = (sub_w == 5) & (lane_w == 0)
    last = summed[base : base + 8]
    square = summed[:base] * summed[:base]
    total = jnp.sum(jnp.sum(square, axis=0, keepdims=True), axis=1, keepdims=True)
    rest = jnp.where(is_loss, 0.0, last * last)
    total = total + jnp.sum(jnp.sum(rest, axis=0, keepdims=True), axis=1, keepdims=True)
    scale = 1.0 / jnp.sqrt(total / number + eps_norm)
    w2_out[...] = summed[:HID] * scale
    for i in range(9):
        w1_out[5 * i : 5 * i + 5] = summed[HID + 8 * i : HID + 8 * i + 5] * scale
    b1_out[...] = summed[HID + 72 : HID + 73] * scale
    w3_out[...] = (summed[HID + FROWS : HID + FROWS + 8] * scale).T[:, :5]
    b2_out[...] = summed[HID + FROWS + 8 : HID + FROWS + 9] * scale
    b3_out[...] = (last * scale)[:, :1]
    loss_out[...] = last[5:6, :1] / cells_total

    for side in range(2):
        @pl.when(remote(side))
        def _(side=side):
            back(side, side).wait()

    def drain(step, carry):
        scatter(step).wait_send()
        gather(step).wait_send()
        return carry

    loop(drain, 0)


def on_device(state, target, depth, land_mask, w_one, b_one, w_two, b_two, w_three, b_three):
    half = lax.axis_index("lat")
    halves = lax.axis_size("lat")
    peers = lax.axis_size("lon") * halves
    cells_lon, cells_lat = depth.shape
    row = cells_lat * halves
    lines = cells_lon // halves
    lanes = lines * row
    ocean = (1 - land_mask).astype(f32)
    zero = jnp.zeros((1, cells_lon, cells_lat), f32)
    block = jnp.concatenate(
        [state, depth[None], ocean[None], zero, target, jnp.zeros((3, cells_lon, cells_lat), f32)], axis=0
    )
    block = jnp.concatenate(
        [jnp.where(half == 0, block, 0.0), jnp.where(half == 1, block, 0.0)], axis=2
    )
    fields = block.reshape(16, halves, lanes).transpose(1, 0, 2)
    number = w_one.size + b_one.size + w_two.size + b_two.size + w_three.size + b_three.size
    used = HID + FROWS + 24
    chunk = -(-used // peers)
    chunk = -(-chunk // 8) * 8
    shape = jax.ShapeDtypeStruct
    vmem = pl.BlockSpec(memory_space=pltpu.VMEM)
    dma = pltpu.SemaphoreType.DMA
    cells_total = peers // halves * cells_lon * row
    outs = pl.pallas_call(
        functools.partial(kernel, peers, chunk, row, float(number), float(cells_total)),
        out_shape=(
            shape((1, 1), f32), shape((2, 8, lanes), f32), shape((45, HID), f32), shape((1, HID), f32),
            shape((HID, HID), f32), shape((1, HID), f32), shape((HID, 5), f32), shape((8, 1), f32),
        ),
        in_specs=[vmem] * 7,
        out_specs=(vmem,) * 8,
        scratch_shapes=[
            pltpu.VMEM((FROWS, HID), f32),
            pltpu.VMEM((HID, 128), f32),
            pltpu.VMEM((HID, 128), f32),
            pltpu.VMEM((8, lanes), f32),
            pltpu.VMEM((2, 16, lanes), f32),
            pltpu.VMEM((2 * LEVELS, 2, 8, 128), f32),
            pltpu.VMEM((2 * LEVELS, 2, 8, 128), f32),
            pltpu.VMEM((LEVELS, FROWS, lanes), f32),
            pltpu.VMEM((LEVELS, HID, lanes), f32),
            pltpu.VMEM((LEVELS, HID, lanes), f32),
            pltpu.VMEM((HID, 3 * FROWS), bf16),
            pltpu.VMEM((FROWS, 3 * HID), bf16),
            pltpu.VMEM((HID, 3 * HID), bf16),
            pltpu.VMEM((HID, 3 * HID), bf16),
            pltpu.VMEM((16, 3 * HID), bf16),
            pltpu.VMEM((HID, 32), bf16),
            pltpu.VMEM((FROWS, HID), f32),
            pltpu.VMEM((HID, HID), f32),
            pltpu.VMEM((8, HID), f32),
            pltpu.VMEM((HID, 128), f32),
            pltpu.VMEM((8, 128), f32),
            pltpu.VMEM((peers, chunk, HID), f32),
            pltpu.VMEM((peers, chunk, HID), f32),
            pltpu.VMEM((peers, chunk, HID), f32),
            dma((2,)),
            dma((2,)),
            dma((2 * LEVELS, 2)),
            dma((2 * LEVELS, 2)),
            dma((2,)),
            dma((2,)),
            dma((peers,)),
            dma((peers,)),
            dma((peers,)),
            dma((peers,)),
        ],
        compiler_params=pltpu.CompilerParams(
            collective_id=0, has_side_effects=True, vmem_limit_bytes=40 * 1024 * 1024
        ),
    )(fields, w_one, b_one[None], w_two, b_two[None], w_three, b_three[None])
    loss, adjoint, d1, e1, d2, e2, d3, e3 = outs
    adjoint = adjoint[:, :5].reshape(2, 5, lines, row).transpose(1, 0, 2, 3).reshape(5, cells_lon, row)
    adjoint = jnp.where(half == 0, adjoint[:, :, :cells_lat], adjoint[:, :, cells_lat:])
    return (
        loss.reshape(1), adjoint, d1, e1.reshape(HID), d2, e2.reshape(HID), d3, e3[:5, 0],
    )


def solution(mesh):
    in_specs = (
        P(None, ("grp", "lon"), "lat"),
        P(None, ("grp", "lon"), "lat"),
        P(("grp", "lon"), "lat"),
        P(("grp", "lon"), "lat"),
    ) + (P(),) * 6
    out_specs = (
        P("grp"),
        P(None, ("grp", "lon"), "lat"),
        P("grp", None),
        P("grp"),
        P("grp", None),
        P("grp"),
        P("grp", None),
        P("grp"),
    )
    return jax.shard_map(
        on_device, mesh=mesh, in_specs=in_specs, out_specs=out_specs, check_vma=False
    )
```

```python
import functools

import jax
import jax.numpy as jnp
from jax import lax
from jax.experimental import pallas as pl
from jax.experimental.pallas import tpu as pltpu
from jax.sharding import PartitionSpec as P

STEPS = 2
LEVELS = 3 * STEPS
HID = 256
FROWS = 80
time_step = 0.4
eps_norm = 1e-06
f32 = jnp.float32
bf16 = jnp.bfloat16
MESH = pl.DeviceIdType.MESH


def split(value):
    high = value.astype(bf16)
    low = (value - high.astype(f32)).astype(bf16)
    return high, low


def matmul(left, right):
    return jnp.dot(left, right, preferred_element_type=f32)


def matmul_t(left, right):
    return lax.dot_general(left, right, (((1,), (1,)), ((), ())), preferred_element_type=f32)


def stacked(value):
    high, low = split(value)
    return jnp.concatenate([high, low, high], axis=0)


def kernel(
    peers, chunk, row, number, cells_total,
    field_ref, w1_ref, b1_ref, w2_ref, b2_ref, w3_ref, b3_ref,
    loss_out, adj_out, w1_out, b1_out, w2_out, b2_out, w3_out, b3_out,
    w1_pad, w3_pad, b2_col, adj_src, part_buf, edge_send, edge_recv, tape_f, tape_h1, tape_h2,
    w1_fwd, w1_bwd, w2_fwd, w2_bwd, w3_fwd, w3_bwd,
    acc_w1, acc_w2, acc_w3, acc_b2, acc_b3,
    grad_buf, reduce_buf, gather_buf,
    part_ssem, part_rsem, edge_ssem, edge_rsem, back_ssem, back_rsem, rs_ssem, rs_rsem, ag_ssem, ag_rsem,
):
    grp = lax.axis_index("grp")
    lon = lax.axis_index("lon")
    half = lax.axis_index("lat")
    snake = peers == 16

    def chip_at(spot):
        return jnp.where(spot < 4, 2 * spot, 15 - 2 * spot) if snake else spot

    spot = jnp.where(lon % 2 == 0, lon // 2, 7 - lon // 2) if snake else lon
    me = spot * 2 + half

    def place(position):
        return (grp, chip_at(position // 2), position % 2)

    east = place((me + 1) % peers)
    west = place((me + peers - 1) % peers)

    barrier = pltpu.get_barrier_semaphore()

    def greet(step, carry):
        pl.semaphore_signal(barrier, inc=1, device_id=place((me + step) % peers), device_id_type=MESH)
        return carry

    lax.fori_loop(1, peers, greet, 0, unroll=peers <= 16)
    pl.semaphore_wait(barrier, peers - 1)

    def spread(side):
        return pltpu.make_async_remote_copy(
            src_ref=field_ref.at[side], dst_ref=part_buf.at[half],
            send_sem=part_ssem.at[side], recv_sem=part_rsem.at[half],
            device_id=(grp, chip_at(lon), side), device_id_type=MESH,
        )

    def arrival(side):
        return pltpu.make_async_remote_copy(
            src_ref=field_ref.at[side], dst_ref=part_buf.at[side],
            send_sem=part_ssem.at[side], recv_sem=part_rsem.at[side],
            device_id=(grp, chip_at(lon), side), device_id_type=MESH,
        )

    at_home = spot == lon

    def remote(side):
        return jnp.logical_not(at_home & (half == side))

    def own(side):
        return at_home & (half == side)

    for side in range(2):
        @pl.when(remote(side))
        def _(side=side):
            spread(side).start()

        @pl.when(own(side))
        def _(side=side):
            part_buf[side] = field_ref[side]

    lanes = field_ref.shape[2]
    lane = lax.broadcasted_iota(jnp.int32, (8, lanes), 1)
    sub = lax.broadcasted_iota(jnp.int32, (8, lanes), 0)
    latitude = lane % row
    low_edge = latitude == 0
    high_edge = latitude == row - 1
    lane_tile = lax.broadcasted_iota(jnp.int32, (8, 128), 1)
    lower_half = lane_tile < row
    coriolis = (0.2 + 0.6 * (latitude.astype(f32) + 0.5) / row)[0:1]

    w1_pad[...] = jnp.zeros_like(w1_pad)
    for i in range(9):
        w1_pad[8 * i : 8 * i + 5] = w1_ref[5 * i : 5 * i + 5]
    w1_pad[72:73] = b1_ref[...]
    w3_pad[...] = jnp.zeros_like(w3_pad)
    w3_pad[:, :5] = w3_ref[...]
    b2_col[...] = jnp.broadcast_to(b2_ref[...], (128, HID)).T
    corner = lax.broadcasted_iota(jnp.int32, (8, 5), 0) == lax.broadcasted_iota(jnp.int32, (8, 5), 1)
    bias_three = jnp.sum(jnp.where(corner, b3_ref[...], 0.0), axis=1, keepdims=True)
    w1 = w1_pad[...]
    high, low = split(w1)
    w1_bwd[...] = jnp.concatenate([high, high, low], axis=1)
    high, low = high.astype(f32), low.astype(f32)
    w1_fwd[...] = jnp.concatenate([high, high, low], axis=0).T.astype(bf16)
    w2 = w2_ref[...]
    high, low = split(w2)
    w2_bwd[...] = jnp.concatenate([high, high, low], axis=1)
    high, low = split(w2.T)
    w2_fwd[...] = jnp.concatenate([high, high, low], axis=1)
    w3t = w3_pad[...].T[:16]
    high, low = split(w3t)
    w3_fwd[...] = jnp.concatenate([high, high, low], axis=1)
    high, low = high.astype(f32)[:8], low.astype(f32)[:8]
    w3_bwd[...] = jnp.concatenate([high, high, low, jnp.zeros_like(low)], axis=0).T.astype(bf16)
    acc_w1[...] = jnp.zeros_like(acc_w1)
    acc_w2[...] = jnp.zeros_like(acc_w2)
    acc_w3[...] = jnp.zeros_like(acc_w3)
    acc_b2[...] = jnp.zeros_like(acc_b2)
    acc_b3[...] = jnp.zeros_like(acc_b3)

    for side in range(2):
        @pl.when(remote(side))
        def _(side=side):
            arrival(side).wait()

    merged = part_buf[0] + part_buf[1]
    fields = merged[:8]
    target = merged[8:]
    ocean = fields[6:7]
    state0 = jnp.where(sub < 5, fields * ocean, fields)

    def exchange(stage, to_east, to_west):
        edge_send[stage, 0] = to_east
        edge_send[stage, 1] = to_west
        copies = []
        for side, device in ((0, east), (1, west)):
            copy = pltpu.make_async_remote_copy(
                src_ref=edge_send.at[stage, side], dst_ref=edge_recv.at[stage, side],
                send_sem=edge_ssem.at[stage, side], recv_sem=edge_rsem.at[stage, side],
                device_id=device, device_id_type=MESH,
            )
            copy.start()
            copies.append(copy)
        return copies

    def lat_down(value):
        return jnp.where(low_edge, 0.0, pltpu.roll(value, 1, 1))

    def lat_up(value):
        return jnp.where(high_edge, 0.0, pltpu.roll(value, lanes - 1, 1))

    def factors(level):
        keep = jnp.where(level == 0, 0.0, jnp.where(level == 1, 0.75, 1.0 / 3.0)).astype(f32)
        move = jnp.where(level == 0, 1.0, jnp.where(level == 1, 0.25, 2.0 / 3.0)).astype(f32)
        return keep, move

    outer = lanes + 256

    def evolve(stage, level, around, start, wide):
        width = outer if wide else lanes
        first_lane = 0 if wide else 128

        def cut(value):
            return value[:, first_lane : first_lane + width]

        rows = lax.broadcasted_iota(jnp.int32, (8, width), 0)
        lats = lax.broadcasted_iota(jnp.int32, (8, width), 1) % row

        def south_of(value):
            return jnp.where(lats == 0, 0.0, pltpu.roll(value, 1, 1))

        def north_of(value):
            return jnp.where(lats == row - 1, 0.0, pltpu.roll(value, width - 1, 1))

        current = cut(around)
        start = cut(start)
        groups = []
        for side in (cut(pltpu.roll(around, row, 1)), current, cut(pltpu.roll(around, outer - row, 1))):
            groups += [south_of(side), side, north_of(side)]
        feats = jnp.concatenate(groups + [jnp.where(rows == 0, 1.0, 0.0).astype(f32)], axis=0)
        hidden_one = jnp.tanh(matmul(w1_fwd[...], stacked(feats)))
        hidden_two = jnp.tanh(matmul(w2_fwd[...], stacked(hidden_one)) + b2_col[:, :1])
        low_lane = 128 if wide else 0
        tape_f[stage] = feats[:, low_lane : low_lane + lanes]
        tape_h1[stage] = hidden_one[:, low_lane : low_lane + lanes]
        tape_h2[stage] = hidden_two[:, low_lane : low_lane + lanes]
        closure = matmul(w3_fwd[...], stacked(hidden_two))[:8] + bias_three
        we, ea, so, no = groups[1], groups[7], groups[3], groups[5]
        laplace = ea + we + no + so - 4.0 * current
        dx, dy = ea - we, no - so
        u, v = current[1:2], current[2:3]
        turn = (0.2 + 0.6 * (lats.astype(f32) + 0.5) / row)[0:1]
        rate_h = -0.5 * (ea[5:6] * ea[1:2] - we[5:6] * we[1:2] + no[5:6] * no[2:3] - so[5:6] * so[2:3])
        rate_u = turn * v - 0.5 * dx[0:1] - 0.05 * u + 0.05 * laplace[1:2]
        rate_v = -turn * u - 0.5 * dy[0:1] - 0.05 * v + 0.05 * laplace[2:3]
        rate_t = 0.05 * laplace - 0.5 * (u * dx + v * dy)
        rates = jnp.where(rows == 0, rate_h, jnp.where(rows == 1, rate_u, jnp.where(rows == 2, rate_v, rate_t)))
        rates = (rates + closure) * current[6:7]
        keep, move = factors(level)
        moved = keep * start + move * (current + time_step * rates)
        return jnp.where(rows < 5, moved, current)

    def forward(pair, carry):
        current, start = carry
        stage = 2 * pair
        level, later = stage % 3, (stage + 1) % 3
        for copy in exchange(stage, current[:, lanes - 128 :], current[:, :128]):
            copy.wait()
        around = jnp.concatenate([edge_recv[stage, 0], current, edge_recv[stage, 1]], axis=1)
        start = jnp.where(level == 0, around, start)
        around = evolve(stage, level, around, start, True)
        start = jnp.where(later == 0, around, start)
        return evolve(stage + 1, later, around, start, False), start

    final, _ = lax.fori_loop(0, LEVELS // 2, forward, (state0, jnp.zeros((8, outer), f32)))
    error = jnp.where(sub < 5, final - target, 0.0)
    adjoint = ocean * error
    misfit = 0.5 * jnp.sum(jnp.sum(adjoint * error, axis=1, keepdims=True), axis=0, keepdims=True)

    def backward(index, carry):
        adjoint, start_total = carry
        stage = LEVELS - 1 - index
        slot = LEVELS + index
        level = stage % 3
        keep, move = factors(level)
        start_total = jnp.where(level == 2, 0.0, start_total) + keep * adjoint
        grad = (move * time_step) * adjoint * ocean
        feats = tape_f[stage]
        hidden_one = tape_h1[stage]
        hidden_two = tape_h2[stage]
        high, low = split(grad)
        high, low = high.astype(f32), low.astype(f32)
        grad_stack = jnp.concatenate([high, low, high, jnp.zeros_like(high)], axis=0).astype(bf16)
        dz2 = matmul(w3_bwd[...], grad_stack) * (1.0 - hidden_two * hidden_two)
        dz2_high, dz2_low = split(dz2)
        dz1 = matmul(w2_bwd[...], jnp.concatenate([dz2_high, dz2_low, dz2_high], axis=0)) * (
            1.0 - hidden_one * hidden_one
        )
        dz1_high, dz1_low = split(dz1)
        dfeats = matmul(w1_bwd[...], jnp.concatenate([dz1_high, dz1_low, dz1_high], axis=0))
        we, ea, so, no, ce = feats[8:16], feats[56:64], feats[24:32], feats[40:48], feats[32:40]
        dx, dy = ea - we, no - so
        u, v = ce[1:2], ce[2:3]
        gh, gu, gv = grad[0:1], grad[1:2], grad[2:3]
        gt = jnp.where(sub >= 3, grad, 0.0)
        lap = jnp.where(sub >= 1, 0.05 * grad, 0.0)
        ugt, vgt = u * gt, v * gt
        d_ea = lap - 0.5 * jnp.where(sub == 0, gu, jnp.where(sub == 1, gh * ea[5:6], ugt))
        d_we = lap + 0.5 * jnp.where(sub == 0, gu, jnp.where(sub == 1, gh * we[5:6], ugt))
        d_no = lap - 0.5 * jnp.where(sub == 0, gv, jnp.where(sub == 2, gh * no[5:6], vgt))
        d_so = lap + 0.5 * jnp.where(sub == 0, gv, jnp.where(sub == 2, gh * so[5:6], vgt))
        du = -coriolis * gv - 0.05 * gu - 0.5 * jnp.sum(gt * dx, axis=0, keepdims=True)
        dv = coriolis * gu - 0.05 * gv - 0.5 * jnp.sum(gt * dy, axis=0, keepdims=True)
        d_ce = jnp.where(sub == 1, du, jnp.where(sub == 2, dv, 0.0)) - 4.0 * lap
        part = [dfeats[8 * i : 8 * i + 8] for i in range(9)]
        to_west = lat_up(part[0]) + (part[1] + d_we) + lat_down(part[2])
        to_east = lat_up(part[6]) + (part[7] + d_ea) + lat_down(part[8])
        stay = lat_up(part[3] + d_so) + (part[4] + d_ce) + lat_down(part[5] + d_no)
        to_west = pltpu.roll(to_west, lanes - row, 1)
        to_east = pltpu.roll(to_east, row, 1)
        copies = exchange(
            slot,
            jnp.where(lower_half, to_east[:, :128], 0.0),
            jnp.where(lower_half, 0.0, to_west[:, lanes - 128 :]),
        )
        result = (
            move * adjoint
            + stay
            + jnp.where(lane < row, 0.0, to_east)
            + jnp.where(lane >= lanes - row, 0.0, to_west)
        )
        h1_high, h1_low = split(hidden_one)
        acc_w2[...] += matmul_t(
            jnp.concatenate([h1_high, h1_high, h1_low], axis=1),
            jnp.concatenate([dz2_high, dz2_low, dz2_high], axis=1),
        )
        f_high, f_low = split(feats)
        acc_w1[...] += matmul_t(
            jnp.concatenate([f_high, f_high, f_low], axis=1),
            jnp.concatenate([dz1_high, dz1_low, dz1_high], axis=1),
        )
        h2_high, h2_low = split(hidden_two)
        g16 = jnp.concatenate([grad, jnp.zeros_like(grad)], axis=0)
        g_high, g_low = split(g16)
        acc_w3[...] += matmul_t(
            jnp.concatenate([g_high, g_high, g_low], axis=1),
            jnp.concatenate([h2_high, h2_low, h2_high], axis=1),
        )[:8]
        acc_b2[...] += sum(dz2[:, i : i + 128] for i in range(0, lanes, 128))
        acc_b3[...] += sum(grad[:, i : i + 128] for i in range(0, lanes, 128))
        for copy in copies:
            copy.wait()
        result = jnp.concatenate(
            [result[:, :128] + edge_recv[slot, 0]]
            + [result[:, i : i + 128] for i in range(128, lanes - 128, 128)]
            + [result[:, lanes - 128 :] + edge_recv[slot, 1]],
            axis=1,
        )
        result = jnp.where(level == 0, result + start_total, result)
        return result, start_total

    adjoint, _ = lax.fori_loop(0, LEVELS, backward, (adjoint, jnp.zeros_like(adjoint)))
    adj_src[...] = adjoint * ocean

    f_row = lax.broadcasted_iota(jnp.int32, (FROWS, HID), 0)
    real = ((f_row < 72) & (f_row % 8 < 5)) | (f_row == 72)
    sub_w = lax.broadcasted_iota(jnp.int32, (8, HID), 0)
    lane_w = lax.broadcasted_iota(jnp.int32, (8, HID), 1)
    b2_row = jnp.sum(acc_b2[...].T, axis=0, keepdims=True)
    b3_col = jnp.sum(acc_b3[...], axis=1, keepdims=True)
    tile_b2 = jnp.where(sub_w == 0, b2_row, 0.0)
    tile_b3 = jnp.where(lane_w == 0, jnp.where(sub_w == 5, misfit, jnp.where(sub_w < 5, b3_col, 0.0)), 0.0)
    extra = peers * chunk - (HID + FROWS + 24)
    pieces = [acc_w2[...], jnp.where(real, acc_w1[...], 0.0), acc_w3[...], tile_b2, tile_b3]
    if extra:
        pieces.append(jnp.zeros((extra, HID), f32))
    grad_buf[...] = jnp.concatenate(pieces, axis=0).reshape(peers, chunk, HID)

    def back(side, slot):
        return pltpu.make_async_remote_copy(
            src_ref=adj_src, dst_ref=adj_out.at[slot],
            send_sem=back_ssem.at[side], recv_sem=back_rsem.at[slot],
            device_id=(grp, spot, side), device_id_type=MESH,
        )

    def scatter(step):
        to = (me + step) % peers
        return pltpu.make_async_remote_copy(
            src_ref=grad_buf.at[to], dst_ref=reduce_buf.at[step],
            send_sem=rs_ssem.at[step], recv_sem=rs_rsem.at[step],
            device_id=place(to), device_id_type=MESH,
        )

    def gather(step):
        to = (me + step) % peers
        return pltpu.make_async_remote_copy(
            src_ref=gather_buf.at[me], dst_ref=gather_buf.at[me],
            send_sem=ag_ssem.at[step], recv_sem=ag_rsem.at[step],
            device_id=place(to), device_id_type=MESH,
        )

    def loop(body, init):
        return lax.fori_loop(1, peers, body, init, unroll=peers <= 16)

    def start_of(make):
        def body(step, carry):
            make(step).start()
            return carry

        return body

    loop(start_of(scatter), 0)
    for side in range(2):
        @pl.when(remote(side))
        def _(side=side):
            back(side, half).start()

        @pl.when(own(side))
        def _(side=side):
            adj_out[side] = adj_src[...]

    def take(step, total):
        scatter(step).wait_recv()
        return total + reduce_buf[step]

    gather_buf[me] = loop(take, grad_buf[me])
    loop(start_of(gather), 0)

    def arrive(step, carry):
        source = (me + peers - step) % peers
        pltpu.make_async_remote_copy(
            src_ref=gather_buf.at[source], dst_ref=gather_buf.at[source],
            send_sem=ag_ssem.at[step], recv_sem=ag_rsem.at[step],
            device_id=place((me + step) % peers), device_id_type=MESH,
        ).wait_recv()
        return carry

    loop(arrive, 0)
    summed = gather_buf[...].reshape(peers * chunk, HID)
    base = HID + FROWS + 16
    is_loss = (sub_w == 5) & (lane_w == 0)
    last = summed[base : base + 8]
    square = summed[:base] * summed[:base]
    total = jnp.sum(jnp.sum(square, axis=0, keepdims=True), axis=1, keepdims=True)
    rest = jnp.where(is_loss, 0.0, last * last)
    total = total + jnp.sum(jnp.sum(rest, axis=0, keepdims=True), axis=1, keepdims=True)
    scale = 1.0 / jnp.sqrt(total / number + eps_norm)
    w2_out[...] = summed[:HID] * scale
    for i in range(9):
        w1_out[5 * i : 5 * i + 5] = summed[HID + 8 * i : HID + 8 * i + 5] * scale
    b1_out[...] = summed[HID + 72 : HID + 73] * scale
    w3_out[...] = (summed[HID + FROWS : HID + FROWS + 8] * scale).T[:, :5]
    b2_out[...] = summed[HID + FROWS + 8 : HID + FROWS + 9] * scale
    b3_out[...] = (last * scale)[:, :1]
    loss_out[...] = last[5:6, :1] / cells_total

    for side in range(2):
        @pl.when(remote(side))
        def _(side=side):
            back(side, side).wait()

    def drain(step, carry):
        scatter(step).wait_send()
        gather(step).wait_send()
        return carry

    loop(drain, 0)


def on_device(state, target, depth, land_mask, w_one, b_one, w_two, b_two, w_three, b_three):
    half = lax.axis_index("lat")
    halves = lax.axis_size("lat")
    peers = lax.axis_size("lon") * halves
    cells_lon, cells_lat = depth.shape
    row = cells_lat * halves
    lines = cells_lon // halves
    lanes = lines * row
    ocean = (1 - land_mask).astype(f32)
    zero = jnp.zeros((1, cells_lon, cells_lat), f32)
    block = jnp.concatenate(
        [state, depth[None], ocean[None], zero, target, jnp.zeros((3, cells_lon, cells_lat), f32)], axis=0
    )
    block = jnp.concatenate(
        [jnp.where(half == 0, block, 0.0), jnp.where(half == 1, block, 0.0)], axis=2
    )
    fields = block.reshape(16, halves, lanes).transpose(1, 0, 2)
    number = w_one.size + b_one.size + w_two.size + b_two.size + w_three.size + b_three.size
    used = HID + FROWS + 24
    chunk = -(-used // peers)
    chunk = -(-chunk // 8) * 8
    shape = jax.ShapeDtypeStruct
    vmem = pl.BlockSpec(memory_space=pltpu.VMEM)
    dma = pltpu.SemaphoreType.DMA
    cells_total = peers // halves * cells_lon * row
    outs = pl.pallas_call(
        functools.partial(kernel, peers, chunk, row, float(number), float(cells_total)),
        out_shape=(
            shape((1, 1), f32), shape((2, 8, lanes), f32), shape((45, HID), f32), shape((1, HID), f32),
            shape((HID, HID), f32), shape((1, HID), f32), shape((HID, 5), f32), shape((8, 1), f32),
        ),
        in_specs=[vmem] * 7,
        out_specs=(vmem,) * 8,
        scratch_shapes=[
            pltpu.VMEM((FROWS, HID), f32),
            pltpu.VMEM((HID, 128), f32),
            pltpu.VMEM((HID, 128), f32),
            pltpu.VMEM((8, lanes), f32),
            pltpu.VMEM((2, 16, lanes), f32),
            pltpu.VMEM((2 * LEVELS, 2, 8, 128), f32),
            pltpu.VMEM((2 * LEVELS, 2, 8, 128), f32),
            pltpu.VMEM((LEVELS, FROWS, lanes), f32),
            pltpu.VMEM((LEVELS, HID, lanes), f32),
            pltpu.VMEM((LEVELS, HID, lanes), f32),
            pltpu.VMEM((HID, 3 * FROWS), bf16),
            pltpu.VMEM((FROWS, 3 * HID), bf16),
            pltpu.VMEM((HID, 3 * HID), bf16),
            pltpu.VMEM((HID, 3 * HID), bf16),
            pltpu.VMEM((16, 3 * HID), bf16),
            pltpu.VMEM((HID, 32), bf16),
            pltpu.VMEM((FROWS, HID), f32),
            pltpu.VMEM((HID, HID), f32),
            pltpu.VMEM((8, HID), f32),
            pltpu.VMEM((HID, 128), f32),
            pltpu.VMEM((8, 128), f32),
            pltpu.VMEM((peers, chunk, HID), f32),
            pltpu.VMEM((peers, chunk, HID), f32),
            pltpu.VMEM((peers, chunk, HID), f32),
            dma((2,)),
            dma((2,)),
            dma((2 * LEVELS, 2)),
            dma((2 * LEVELS, 2)),
            dma((2,)),
            dma((2,)),
            dma((peers,)),
            dma((peers,)),
            dma((peers,)),
            dma((peers,)),
        ],
        compiler_params=pltpu.CompilerParams(
            collective_id=0, has_side_effects=True, vmem_limit_bytes=40 * 1024 * 1024
        ),
    )(fields, w_one, b_one[None], w_two, b_two[None], w_three, b_three[None])
    loss, adjoint, d1, e1, d2, e2, d3, e3 = outs
    adjoint = adjoint[:, :5].reshape(2, 5, lines, row).transpose(1, 0, 2, 3).reshape(5, cells_lon, row)
    adjoint = jnp.where(half == 0, adjoint[:, :, :cells_lat], adjoint[:, :, cells_lat:])
    return (
        loss.reshape(1), adjoint, d1, e1.reshape(HID), d2, e2.reshape(HID), d3, e3[:5, 0],
    )


def solution(mesh):
    in_specs = (
        P(None, ("grp", "lon"), "lat"),
        P(None, ("grp", "lon"), "lat"),
        P(("grp", "lon"), "lat"),
        P(("grp", "lon"), "lat"),
    ) + (P(),) * 6
    out_specs = (
        P("grp"),
        P(None, ("grp", "lon"), "lat"),
        P("grp", None),
        P("grp"),
        P("grp", None),
        P("grp"),
        P("grp", None),
        P("grp"),
    )
    return jax.shard_map(
        on_device, mesh=mesh, in_specs=in_specs, out_specs=out_specs, check_vma=False
    )
```

```python
import functools

import jax
import jax.numpy as jnp
from jax import lax
from jax.experimental import pallas as pl
from jax.experimental.pallas import tpu as pltpu
from jax.sharding import PartitionSpec as P

STEPS = 2
LEVELS = 3 * STEPS
HID = 256
FROWS = 80
time_step = 0.4
eps_norm = 1e-06
f32 = jnp.float32
bf16 = jnp.bfloat16
MESH = pl.DeviceIdType.MESH


def split(value):
    high = value.astype(bf16)
    low = (value - high.astype(f32)).astype(bf16)
    return high, low


def matmul(left, right):
    return jnp.dot(left, right, preferred_element_type=f32)


def matmul_t(left, right):
    return lax.dot_general(left, right, (((1,), (1,)), ((), ())), preferred_element_type=f32)


def stacked(value):
    high, low = split(value)
    return jnp.concatenate([high, low, high], axis=0)


def kernel(
    peers, chunk, row, number, cells_total,
    field_ref, w1_ref, b1_ref, w2_ref, b2_ref, w3_ref, b3_ref,
    loss_out, block_out, w1_out, b1_out, w2_out, b2_out, w3_out, b3_out,
    w1_pad, w3_pad, b2_col, adj_out, adj_src, part_buf, edge_send, edge_recv, tape_f, tape_h1, tape_h2,
    w1_fwd, w1_bwd, w2_fwd, w2_bwd, w3_fwd, w3_bwd,
    acc_w1, acc_w2, acc_w3, acc_b2, acc_b3,
    grad_buf, reduce_buf, gather_buf,
    part_ssem, part_rsem, edge_ssem, edge_rsem, back_ssem, back_rsem, rs_ssem, rs_rsem, ag_ssem, ag_rsem,
):
    grp = lax.axis_index("grp")
    lon = lax.axis_index("lon")
    half = lax.axis_index("lat")
    snake = peers == 16

    def chip_at(spot):
        return jnp.where(spot < 4, 2 * spot, 15 - 2 * spot) if snake else spot

    spot = jnp.where(lon % 2 == 0, lon // 2, 7 - lon // 2) if snake else lon
    me = spot * 2 + half

    def place(position):
        return (grp, chip_at(position // 2), position % 2)

    east = place((me + 1) % peers)
    west = place((me + peers - 1) % peers)

    barrier = pltpu.get_barrier_semaphore()

    def greet(step, carry):
        pl.semaphore_signal(barrier, inc=1, device_id=place((me + step) % peers), device_id_type=MESH)
        return carry

    lax.fori_loop(1, peers, greet, 0, unroll=peers <= 16)
    pl.semaphore_wait(barrier, peers - 1)

    def spread(side):
        return pltpu.make_async_remote_copy(
            src_ref=field_ref.at[side], dst_ref=part_buf.at[half],
            send_sem=part_ssem.at[side], recv_sem=part_rsem.at[half],
            device_id=(grp, chip_at(lon), side), device_id_type=MESH,
        )

    def arrival(side):
        return pltpu.make_async_remote_copy(
            src_ref=field_ref.at[side], dst_ref=part_buf.at[side],
            send_sem=part_ssem.at[side], recv_sem=part_rsem.at[side],
            device_id=(grp, chip_at(lon), side), device_id_type=MESH,
        )

    at_home = spot == lon

    def remote(side):
        return jnp.logical_not(at_home & (half == side))

    def own(side):
        return at_home & (half == side)

    for side in range(2):
        @pl.when(remote(side))
        def _(side=side):
            spread(side).start()

        @pl.when(own(side))
        def _(side=side):
            part_buf[side] = field_ref[side]

    lanes = field_ref.shape[2]
    lane = lax.broadcasted_iota(jnp.int32, (8, lanes), 1)
    sub = lax.broadcasted_iota(jnp.int32, (8, lanes), 0)
    latitude = lane % row
    low_edge = latitude == 0
    high_edge = latitude == row - 1
    lane_tile = lax.broadcasted_iota(jnp.int32, (8, 128), 1)
    lower_half = lane_tile < row
    coriolis = (0.2 + 0.6 * (latitude.astype(f32) + 0.5) / row)[0:1]

    w1_pad[...] = jnp.zeros_like(w1_pad)
    for i in range(9):
        w1_pad[8 * i : 8 * i + 5] = w1_ref[5 * i : 5 * i + 5]
    w1_pad[72:73] = b1_ref[...]
    w3_pad[...] = jnp.zeros_like(w3_pad)
    w3_pad[:, :5] = w3_ref[...]
    b2_col[...] = jnp.broadcast_to(b2_ref[...], (128, HID)).T
    corner = lax.broadcasted_iota(jnp.int32, (8, 5), 0) == lax.broadcasted_iota(jnp.int32, (8, 5), 1)
    bias_three = jnp.sum(jnp.where(corner, b3_ref[...], 0.0), axis=1, keepdims=True)
    w1 = w1_pad[...]
    high, low = split(w1)
    w1_bwd[...] = jnp.concatenate([high, high, low], axis=1)
    high, low = high.astype(f32), low.astype(f32)
    w1_fwd[...] = jnp.concatenate([high, high, low], axis=0).T.astype(bf16)
    w2 = w2_ref[...]
    high, low = split(w2)
    w2_bwd[...] = jnp.concatenate([high, high, low], axis=1)
    high, low = split(w2.T)
    w2_fwd[...] = jnp.concatenate([high, high, low], axis=1)
    w3t = w3_pad[...].T[:16]
    high, low = split(w3t)
    w3_fwd[...] = jnp.concatenate([high, high, low], axis=1)
    high, low = high.astype(f32)[:8], low.astype(f32)[:8]
    w3_bwd[...] = jnp.concatenate([high, high, low, jnp.zeros_like(low)], axis=0).T.astype(bf16)
    acc_w1[...] = jnp.zeros_like(acc_w1)
    acc_w2[...] = jnp.zeros_like(acc_w2)
    acc_w3[...] = jnp.zeros_like(acc_w3)
    acc_b2[...] = jnp.zeros_like(acc_b2)
    acc_b3[...] = jnp.zeros_like(acc_b3)

    for side in range(2):
        @pl.when(remote(side))
        def _(side=side):
            arrival(side).wait()

    merged = part_buf[0] + part_buf[1]
    fields = merged[:8]
    target = merged[8:]
    ocean = fields[6:7]
    state0 = jnp.where(sub < 5, fields * ocean, fields)

    def exchange(stage, to_east, to_west):
        edge_send[stage, 0] = to_east
        edge_send[stage, 1] = to_west
        copies = []
        for side, device in ((0, east), (1, west)):
            copy = pltpu.make_async_remote_copy(
                src_ref=edge_send.at[stage, side], dst_ref=edge_recv.at[stage, side],
                send_sem=edge_ssem.at[stage, side], recv_sem=edge_rsem.at[stage, side],
                device_id=device, device_id_type=MESH,
            )
            copy.start()
            copies.append(copy)
        return copies

    def lat_down(value):
        return jnp.where(low_edge, 0.0, pltpu.roll(value, 1, 1))

    def lat_up(value):
        return jnp.where(high_edge, 0.0, pltpu.roll(value, lanes - 1, 1))

    def factors(level):
        keep = jnp.where(level == 0, 0.0, jnp.where(level == 1, 0.75, 1.0 / 3.0)).astype(f32)
        move = jnp.where(level == 0, 1.0, jnp.where(level == 1, 0.25, 2.0 / 3.0)).astype(f32)
        return keep, move

    outer = lanes + 256

    def evolve(stage, level, around, start, wide):
        width = outer if wide else lanes
        first_lane = 0 if wide else 128

        def cut(value):
            return value[:, first_lane : first_lane + width]

        rows = lax.broadcasted_iota(jnp.int32, (8, width), 0)
        lats = lax.broadcasted_iota(jnp.int32, (8, width), 1) % row

        def south_of(value):
            return jnp.where(lats == 0, 0.0, pltpu.roll(value, 1, 1))

        def north_of(value):
            return jnp.where(lats == row - 1, 0.0, pltpu.roll(value, width - 1, 1))

        current = cut(around)
        start = cut(start)
        groups = []
        for side in (cut(pltpu.roll(around, row, 1)), current, cut(pltpu.roll(around, outer - row, 1))):
            groups += [south_of(side), side, north_of(side)]
        feats = jnp.concatenate(groups + [jnp.where(rows == 0, 1.0, 0.0).astype(f32)], axis=0)
        hidden_one = jnp.tanh(matmul(w1_fwd[...], stacked(feats)))
        hidden_two = jnp.tanh(matmul(w2_fwd[...], stacked(hidden_one)) + b2_col[:, :1])
        low_lane = 128 if wide else 0
        tape_f[stage] = feats[:, low_lane : low_lane + lanes]
        tape_h1[stage] = hidden_one[:, low_lane : low_lane + lanes]
        tape_h2[stage] = hidden_two[:, low_lane : low_lane + lanes]
        closure = matmul(w3_fwd[...], stacked(hidden_two))[:8] + bias_three
        we, ea, so, no = groups[1], groups[7], groups[3], groups[5]
        laplace = ea + we + no + so - 4.0 * current
        dx, dy = ea - we, no - so
        u, v = current[1:2], current[2:3]
        turn = (0.2 + 0.6 * (lats.astype(f32) + 0.5) / row)[0:1]
        rate_h = -0.5 * (ea[5:6] * ea[1:2] - we[5:6] * we[1:2] + no[5:6] * no[2:3] - so[5:6] * so[2:3])
        rate_u = turn * v - 0.5 * dx[0:1] - 0.05 * u + 0.05 * laplace[1:2]
        rate_v = -turn * u - 0.5 * dy[0:1] - 0.05 * v + 0.05 * laplace[2:3]
        rate_t = 0.05 * laplace - 0.5 * (u * dx + v * dy)
        rates = jnp.where(rows == 0, rate_h, jnp.where(rows == 1, rate_u, jnp.where(rows == 2, rate_v, rate_t)))
        rates = (rates + closure) * current[6:7]
        keep, move = factors(level)
        moved = keep * start + move * (current + time_step * rates)
        return jnp.where(rows < 5, moved, current)

    def forward(pair, carry):
        current, start = carry
        stage = 2 * pair
        level, later = stage % 3, (stage + 1) % 3
        for copy in exchange(stage, current[:, lanes - 128 :], current[:, :128]):
            copy.wait()
        around = jnp.concatenate([edge_recv[stage, 0], current, edge_recv[stage, 1]], axis=1)
        start = jnp.where(level == 0, around, start)
        around = evolve(stage, level, around, start, True)
        start = jnp.where(later == 0, around, start)
        return evolve(stage + 1, later, around, start, False), start

    final, _ = lax.fori_loop(0, LEVELS // 2, forward, (state0, jnp.zeros((8, outer), f32)))
    error = jnp.where(sub < 5, final - target, 0.0)
    adjoint = ocean * error
    misfit = 0.5 * jnp.sum(jnp.sum(adjoint * error, axis=1, keepdims=True), axis=0, keepdims=True)

    def backward(index, carry):
        adjoint, start_total = carry
        stage = LEVELS - 1 - index
        slot = LEVELS + index
        level = stage % 3
        keep, move = factors(level)
        start_total = jnp.where(level == 2, 0.0, start_total) + keep * adjoint
        grad = (move * time_step) * adjoint * ocean
        feats = tape_f[stage]
        hidden_one = tape_h1[stage]
        hidden_two = tape_h2[stage]
        high, low = split(grad)
        high, low = high.astype(f32), low.astype(f32)
        grad_stack = jnp.concatenate([high, low, high, jnp.zeros_like(high)], axis=0).astype(bf16)
        dz2 = matmul(w3_bwd[...], grad_stack) * (1.0 - hidden_two * hidden_two)
        dz2_high, dz2_low = split(dz2)
        dz1 = matmul(w2_bwd[...], jnp.concatenate([dz2_high, dz2_low, dz2_high], axis=0)) * (
            1.0 - hidden_one * hidden_one
        )
        dz1_high, dz1_low = split(dz1)
        dfeats = matmul(w1_bwd[...], jnp.concatenate([dz1_high, dz1_low, dz1_high], axis=0))
        we, ea, so, no, ce = feats[8:16], feats[56:64], feats[24:32], feats[40:48], feats[32:40]
        dx, dy = ea - we, no - so
        u, v = ce[1:2], ce[2:3]
        gh, gu, gv = grad[0:1], grad[1:2], grad[2:3]
        gt = jnp.where(sub >= 3, grad, 0.0)
        lap = jnp.where(sub >= 1, 0.05 * grad, 0.0)
        ugt, vgt = u * gt, v * gt
        d_ea = lap - 0.5 * jnp.where(sub == 0, gu, jnp.where(sub == 1, gh * ea[5:6], ugt))
        d_we = lap + 0.5 * jnp.where(sub == 0, gu, jnp.where(sub == 1, gh * we[5:6], ugt))
        d_no = lap - 0.5 * jnp.where(sub == 0, gv, jnp.where(sub == 2, gh * no[5:6], vgt))
        d_so = lap + 0.5 * jnp.where(sub == 0, gv, jnp.where(sub == 2, gh * so[5:6], vgt))
        du = -coriolis * gv - 0.05 * gu - 0.5 * jnp.sum(gt * dx, axis=0, keepdims=True)
        dv = coriolis * gu - 0.05 * gv - 0.5 * jnp.sum(gt * dy, axis=0, keepdims=True)
        d_ce = jnp.where(sub == 1, du, jnp.where(sub == 2, dv, 0.0)) - 4.0 * lap
        part = [dfeats[8 * i : 8 * i + 8] for i in range(9)]
        to_west = lat_up(part[0]) + (part[1] + d_we) + lat_down(part[2])
        to_east = lat_up(part[6]) + (part[7] + d_ea) + lat_down(part[8])
        stay = lat_up(part[3] + d_so) + (part[4] + d_ce) + lat_down(part[5] + d_no)
        to_west = pltpu.roll(to_west, lanes - row, 1)
        to_east = pltpu.roll(to_east, row, 1)
        copies = exchange(
            slot,
            jnp.where(lower_half, to_east[:, :128], 0.0),
            jnp.where(lower_half, 0.0, to_west[:, lanes - 128 :]),
        )
        result = (
            move * adjoint
            + stay
            + jnp.where(lane < row, 0.0, to_east)
            + jnp.where(lane >= lanes - row, 0.0, to_west)
        )
        h1_high, h1_low = split(hidden_one)
        acc_w2[...] += matmul_t(
            jnp.concatenate([h1_high, h1_high, h1_low], axis=1),
            jnp.concatenate([dz2_high, dz2_low, dz2_high], axis=1),
        )
        f_high, f_low = split(feats)
        acc_w1[...] += matmul_t(
            jnp.concatenate([f_high, f_high, f_low], axis=1),
            jnp.concatenate([dz1_high, dz1_low, dz1_high], axis=1),
        )
        h2_high, h2_low = split(hidden_two)
        g16 = jnp.concatenate([grad, jnp.zeros_like(grad)], axis=0)
        g_high, g_low = split(g16)
        acc_w3[...] += matmul_t(
            jnp.concatenate([g_high, g_high, g_low], axis=1),
            jnp.concatenate([h2_high, h2_low, h2_high], axis=1),
        )[:8]
        acc_b2[...] += sum(dz2[:, i : i + 128] for i in range(0, lanes, 128))
        acc_b3[...] += sum(grad[:, i : i + 128] for i in range(0, lanes, 128))
        for copy in copies:
            copy.wait()
        result = jnp.concatenate(
            [result[:, :128] + edge_recv[slot, 0]]
            + [result[:, i : i + 128] for i in range(128, lanes - 128, 128)]
            + [result[:, lanes - 128 :] + edge_recv[slot, 1]],
            axis=1,
        )
        result = jnp.where(level == 0, result + start_total, result)
        return result, start_total

    adjoint, _ = lax.fori_loop(0, LEVELS, backward, (adjoint, jnp.zeros_like(adjoint)))
    adj_src[...] = adjoint * ocean

    f_row = lax.broadcasted_iota(jnp.int32, (FROWS, HID), 0)
    real = ((f_row < 72) & (f_row % 8 < 5)) | (f_row == 72)
    sub_w = lax.broadcasted_iota(jnp.int32, (8, HID), 0)
    lane_w = lax.broadcasted_iota(jnp.int32, (8, HID), 1)
    b2_row = jnp.sum(acc_b2[...].T, axis=0, keepdims=True)
    b3_col = jnp.sum(acc_b3[...], axis=1, keepdims=True)
    tile_b2 = jnp.where(sub_w == 0, b2_row, 0.0)
    tile_b3 = jnp.where(lane_w == 0, jnp.where(sub_w == 5, misfit, jnp.where(sub_w < 5, b3_col, 0.0)), 0.0)
    extra = peers * chunk - (HID + FROWS + 24)
    pieces = [acc_w2[...], jnp.where(real, acc_w1[...], 0.0), acc_w3[...], tile_b2, tile_b3]
    if extra:
        pieces.append(jnp.zeros((extra, HID), f32))
    grad_buf[...] = jnp.concatenate(pieces, axis=0).reshape(peers, chunk, HID)

    def back(side, slot):
        return pltpu.make_async_remote_copy(
            src_ref=adj_src, dst_ref=adj_out.at[slot],
            send_sem=back_ssem.at[side], recv_sem=back_rsem.at[slot],
            device_id=(grp, spot, side), device_id_type=MESH,
        )

    def scatter(step):
        to = (me + step) % peers
        return pltpu.make_async_remote_copy(
            src_ref=grad_buf.at[to], dst_ref=reduce_buf.at[step],
            send_sem=rs_ssem.at[step], recv_sem=rs_rsem.at[step],
            device_id=place(to), device_id_type=MESH,
        )

    def gather(step):
        to = (me + step) % peers
        return pltpu.make_async_remote_copy(
            src_ref=gather_buf.at[me], dst_ref=gather_buf.at[me],
            send_sem=ag_ssem.at[step], recv_sem=ag_rsem.at[step],
            device_id=place(to), device_id_type=MESH,
        )

    def loop(body, init):
        return lax.fori_loop(1, peers, body, init, unroll=peers <= 16)

    def start_of(make):
        def body(step, carry):
            make(step).start()
            return carry

        return body

    loop(start_of(scatter), 0)
    for side in range(2):
        @pl.when(remote(side))
        def _(side=side):
            back(side, half).start()

        @pl.when(own(side))
        def _(side=side):
            adj_out[side] = adj_src[...]

    def take(step, total):
        scatter(step).wait_recv()
        return total + reduce_buf[step]

    gather_buf[me] = loop(take, grad_buf[me])
    loop(start_of(gather), 0)

    def arrive(step, carry):
        source = (me + peers - step) % peers
        pltpu.make_async_remote_copy(
            src_ref=gather_buf.at[source], dst_ref=gather_buf.at[source],
            send_sem=ag_ssem.at[step], recv_sem=ag_rsem.at[step],
            device_id=place((me + step) % peers), device_id_type=MESH,
        ).wait_recv()
        return carry

    loop(arrive, 0)
    summed = gather_buf[...].reshape(peers * chunk, HID)
    base = HID + FROWS + 16
    is_loss = (sub_w == 5) & (lane_w == 0)
    last = summed[base : base + 8]
    square = summed[:base] * summed[:base]
    total = jnp.sum(jnp.sum(square, axis=0, keepdims=True), axis=1, keepdims=True)
    rest = jnp.where(is_loss, 0.0, last * last)
    total = total + jnp.sum(jnp.sum(rest, axis=0, keepdims=True), axis=1, keepdims=True)
    scale = 1.0 / jnp.sqrt(total / number + eps_norm)
    w2_out[...] = summed[:HID] * scale
    for i in range(9):
        w1_out[5 * i : 5 * i + 5] = summed[HID + 8 * i : HID + 8 * i + 5] * scale
    b1_out[...] = summed[HID + 72 : HID + 73] * scale
    w3_out[...] = (summed[HID + FROWS : HID + FROWS + 8] * scale).T[:, :5]
    b2_out[...] = summed[HID + FROWS + 8 : HID + FROWS + 9] * scale
    b3_out[...] = (last * scale)[:, :1]
    loss_out[...] = last[5:6, :1] / cells_total

    for side in range(2):
        @pl.when(remote(side))
        def _(side=side):
            back(side, side).wait()

    lines = lanes // row
    for side in range(2):
        whole = adj_out[side][:5]
        for line in range(lines):
            left = whole[:, line * row : line * row + row // 2]
            right = whole[:, line * row + row // 2 : (line + 1) * row]
            block_out[:, side * lines + line, :] = jnp.where(half == 0, left, right)

    def drain(step, carry):
        scatter(step).wait_send()
        gather(step).wait_send()
        return carry

    loop(drain, 0)


def on_device(state, target, depth, land_mask, w_one, b_one, w_two, b_two, w_three, b_three):
    half = lax.axis_index("lat")
    halves = lax.axis_size("lat")
    peers = lax.axis_size("lon") * halves
    cells_lon, cells_lat = depth.shape
    row = cells_lat * halves
    lines = cells_lon // halves
    lanes = lines * row
    ocean = (1 - land_mask).astype(f32)
    zero = jnp.zeros((1, cells_lon, cells_lat), f32)
    block = jnp.concatenate(
        [state, depth[None], ocean[None], zero, target, jnp.zeros((3, cells_lon, cells_lat), f32)], axis=0
    )
    block = jnp.concatenate(
        [jnp.where(half == 0, block, 0.0), jnp.where(half == 1, block, 0.0)], axis=2
    )
    fields = block.reshape(16, halves, lanes).transpose(1, 0, 2)
    number = w_one.size + b_one.size + w_two.size + b_two.size + w_three.size + b_three.size
    used = HID + FROWS + 24
    chunk = -(-used // peers)
    chunk = -(-chunk // 8) * 8
    shape = jax.ShapeDtypeStruct
    vmem = pl.BlockSpec(memory_space=pltpu.VMEM)
    dma = pltpu.SemaphoreType.DMA
    cells_total = peers // halves * cells_lon * row
    outs = pl.pallas_call(
        functools.partial(kernel, peers, chunk, row, float(number), float(cells_total)),
        out_shape=(
            shape((1, 1), f32), shape((5, cells_lon, cells_lat), f32), shape((45, HID), f32), shape((1, HID), f32),
            shape((HID, HID), f32), shape((1, HID), f32), shape((HID, 5), f32), shape((8, 1), f32),
        ),
        in_specs=[vmem] * 7,
        out_specs=(vmem,) * 8,
        scratch_shapes=[
            pltpu.VMEM((FROWS, HID), f32),
            pltpu.VMEM((HID, 128), f32),
            pltpu.VMEM((HID, 128), f32),
            pltpu.VMEM((2, 8, lanes), f32),
            pltpu.VMEM((8, lanes), f32),
            pltpu.VMEM((2, 16, lanes), f32),
            pltpu.VMEM((2 * LEVELS, 2, 8, 128), f32),
            pltpu.VMEM((2 * LEVELS, 2, 8, 128), f32),
            pltpu.VMEM((LEVELS, FROWS, lanes), f32),
            pltpu.VMEM((LEVELS, HID, lanes), f32),
            pltpu.VMEM((LEVELS, HID, lanes), f32),
            pltpu.VMEM((HID, 3 * FROWS), bf16),
            pltpu.VMEM((FROWS, 3 * HID), bf16),
            pltpu.VMEM((HID, 3 * HID), bf16),
            pltpu.VMEM((HID, 3 * HID), bf16),
            pltpu.VMEM((16, 3 * HID), bf16),
            pltpu.VMEM((HID, 32), bf16),
            pltpu.VMEM((FROWS, HID), f32),
            pltpu.VMEM((HID, HID), f32),
            pltpu.VMEM((8, HID), f32),
            pltpu.VMEM((HID, 128), f32),
            pltpu.VMEM((8, 128), f32),
            pltpu.VMEM((peers, chunk, HID), f32),
            pltpu.VMEM((peers, chunk, HID), f32),
            pltpu.VMEM((peers, chunk, HID), f32),
            dma((2,)),
            dma((2,)),
            dma((2 * LEVELS, 2)),
            dma((2 * LEVELS, 2)),
            dma((2,)),
            dma((2,)),
            dma((peers,)),
            dma((peers,)),
            dma((peers,)),
            dma((peers,)),
        ],
        compiler_params=pltpu.CompilerParams(
            collective_id=0, has_side_effects=True, vmem_limit_bytes=40 * 1024 * 1024
        ),
    )(fields, w_one, b_one[None], w_two, b_two[None], w_three, b_three[None])
    loss, adjoint, d1, e1, d2, e2, d3, e3 = outs
    return (
        loss.reshape(1), adjoint, d1, e1.reshape(HID), d2, e2.reshape(HID), d3, e3[:5, 0],
    )


def solution(mesh):
    in_specs = (
        P(None, ("grp", "lon"), "lat"),
        P(None, ("grp", "lon"), "lat"),
        P(("grp", "lon"), "lat"),
        P(("grp", "lon"), "lat"),
    ) + (P(),) * 6
    out_specs = (
        P("grp"),
        P(None, ("grp", "lon"), "lat"),
        P("grp", None),
        P("grp"),
        P("grp", None),
        P("grp"),
        P("grp", None),
        P("grp"),
    )
    return jax.shard_map(
        on_device, mesh=mesh, in_specs=in_specs, out_specs=out_specs, check_vma=False
    )
```
